512 devices in a mesh: dp: 64 (over z_hi, y, core), pre: 8 (over x, z_lo).
Axes of the slice: x: 4, y: 8, z: 8 (z_hi: 4, z_lo: 2; z = z_hi * 2 + z_lo), core: 2. Of those that a mesh axis runs over, the one named last changes fastest.
Arguments:
- inputs: bfloat16 [8192, 4096], P('dp'), may hold values from -12 to 12, as said below
- weight: bfloat16 [4096, 1024], P(None, 'pre'), may hold values from -0.09375 to 0.09375
- cotangent: bfloat16 [8192, 1024], P('dp', 'pre'), may hold values from -12 to 12, as said below
Outputs:
- outputs: bfloat16 [8192, 1024], P('dp', 'pre')
- update: bfloat16 [8, 512, 1024], P(None, 'pre')
The draws below stay inside these ranges and needn't reach their ends.
Inputs may be any that keep to these rules, and one draw needn't show every extreme that they name: `inputs`: activations with unequal scales across features. `cotangent`: gradients with unequal scales across features.
All inputs are finite; a program needn't handle non-finite values.
Results may differ from the reference program's by a relative error of at most 0.0079.
Values may be sent and summed in bfloat16 or wider, within the bound.
A program may use at most 64 MiB of HBM per device.

```python
import math
import jax
import jax.numpy as jnp
from jax import lax

D = 4096
BLOCK = 512
CB = 2
ITERS = 3
C = 1024
RB = 8
TOKENS = 8192


def draw_inputs(key, part):
    key = jax.random.fold_in(key, 11)
    key_base, key_scale = jax.random.split(key, 2)
    base_draw = jax.random.normal(key_base, (TOKENS, D), jnp.float32)
    scales = jnp.exp(jax.random.uniform(key_scale, (1, D), jnp.float32, -1.2, 1.2))
    return jnp.clip(base_draw * scales, -12.0, 12.0).astype(jnp.bfloat16)


def draw_cotangent(key, part):
    key = jax.random.fold_in(key, 23)
    key_base, key_scale = jax.random.split(key, 2)
    base_draw = jax.random.normal(key_base, (TOKENS, CB * BLOCK), jnp.float32)
    scales = jnp.exp(jax.random.uniform(key_scale, (1, CB * BLOCK), jnp.float32, -1.2, 1.2))
    return jnp.clip(base_draw * scales, -12.0, 12.0).astype(jnp.bfloat16)


def block_scale(stream_key, shape, cuts, low, largest):
    loudness = 1.0
    for position, shards_of in cuts:
        steps = jax.random.uniform(jax.random.fold_in(jax.random.fold_in(stream_key, 6), position), (shards_of,), jnp.float32, low / len(cuts), largest / len(cuts))
        loudness = loudness * jnp.repeat(jnp.exp(steps), shape[position] // shards_of).reshape((-1,) + (1,) * (len(shape) - 1 - position))
    return loudness


def bell_draw(stream_key, shape, scale, reach, cuts=(), held_as=jnp.bfloat16):
    level = block_scale(stream_key, shape, cuts, -0.22, 0.18) if cuts else 1.0
    drawn = jax.random.normal(stream_key, shape, jnp.float32) * scale * level
    return jnp.minimum(jnp.maximum(drawn, -reach), reach).astype(held_as)


def setup_inputs(seed: int = 0) -> dict:
    splits = jax.random.split(jax.random.key(seed), 4)
    return {
        "inputs": draw_inputs(jax.random.fold_in(splits[3], 71), 0),
        "weight": bell_draw(splits[1], (D, C), D ** -0.5, 0.09375, ((1, 8),)),
        "cotangent": draw_cotangent(jax.random.fold_in(splits[3], 71), 0),
    }


DAMPING = 0.1
HIGH = lax.Precision.HIGHEST

def inverse_root(statistic):
    order_n = statistic.shape[0]
    unit_eye = jnp.eye(order_n, dtype=jnp.float32)
    damp_shift = DAMPING * jnp.trace(statistic) / order_n
    matrix = statistic + damp_shift * unit_eye
    frob_norm = jnp.sqrt(jnp.sum(matrix * matrix))
    normalized = matrix / frob_norm
    root_now = unit_eye * frob_norm ** (-0.25)
    for iteration in range(ITERS):
        factor = (5.0 * unit_eye - normalized) * 0.25
        square = jnp.dot(factor, factor, precision=HIGH)
        fourth = jnp.dot(square, square, precision=HIGH)
        normalized = jnp.dot(fourth, normalized, precision=HIGH)
        root_now = jnp.dot(root_now, factor, precision=HIGH)
    return root_now

def one_block(grad_block):
    left_stat = jnp.dot(grad_block, grad_block.T, precision=HIGH)
    right_stat = jnp.dot(grad_block.T, grad_block, precision=HIGH)
    root_left = inverse_root(left_stat).astype(jnp.bfloat16)
    root_right = inverse_root(right_stat).astype(jnp.bfloat16)
    half_prod = jnp.dot(root_left, grad_block.astype(jnp.bfloat16), preferred_element_type=jnp.float32).astype(jnp.bfloat16)
    full_prod = jnp.dot(half_prod, root_right, preferred_element_type=jnp.float32)
    return (full_prod * math.sqrt(BLOCK)).astype(jnp.bfloat16)

def reference(inputs, weight, cotangent):
    outputs = jnp.dot(inputs, weight, preferred_element_type=jnp.float32).astype(jnp.bfloat16)
    gradient = jnp.dot(inputs.T, cotangent, preferred_element_type=jnp.float32)
    grad_blocks = gradient.reshape(RB, BLOCK, CB, BLOCK).transpose(0, 2, 1, 3).reshape(RB * CB, BLOCK, BLOCK)
    pieces = lax.map(one_block, grad_blocks)
    update = pieces.reshape(RB, CB, BLOCK, BLOCK).transpose(0, 2, 1, 3).reshape(RB, BLOCK, CB * BLOCK)
    return (outputs, update)
```

```python
import math

import jax
import jax.numpy as jnp
from jax import lax
from jax.experimental import pallas as pl
from jax.experimental.pallas import tpu as pltpu
from jax.sharding import PartitionSpec as P

D = 4096
BLOCK = 512
CB = 2
HALF = BLOCK // 2
DAMPING = 0.1
MESH = pl.DeviceIdType.MESH
BF16 = jnp.bfloat16
F32 = jnp.float32

Y_ORDER = (4, 3, 5, 2, 6, 1, 7, 0)


def nn(a, b):
    return lax.dot_general(a, b, (((1,), (0,)), ((), ())), preferred_element_type=F32)


def nt(a, b):
    return lax.dot_general(a, b, (((1,), (1,)), ((), ())), preferred_element_type=F32)


def kernel(
    a_hbm, w_hbm, b_hbm, out_ref, upd_hbm,
    a_v, w_v, b_v, a_s, b_s, part, rs_buf, tile, u_ref,
    m0, m1, m2, t0, b0, b1, xr, hbuf, rbuf, osrc, oland,
    load_sem, as_send, as_recv, bs_send, bs_recv, rs_send, rs_recv,
    ag_send, ag_recv, th_send, th_recv, ex_send, ex_recv,
    o_send, o_recv, of_send, of_recv, fin_sem,
):
    dp = lax.axis_index("dp")
    pre = lax.axis_index("pre")
    zh, y, core = dp // 16, (dp // 2) % 8, dp % 2
    x, zl = pre // 2, pre % 2
    z = zh * 2 + zl
    c = x // 2
    x_pair = c * 2 + (1 - x % 2)
    x_mirror = 3 - x

    def dev(zh_, y_, core_, x_, zl_):
        return ((zh_ * 8 + y_) * 2 + core_, x_ * 2 + zl_)

    sibling = dev(zh, y, 1 - core, x, zl)

    def rs_peer(dy, dzh):
        return dev((zh + dzh) % 4, (y + dy) % 8, core, x, zl)

    def ag_peer(dx, dz):
        z_ = (z + dz) % 8
        return dev(z_ // 2, y, core, x_pair if dx else x, z_ % 2)

    def out_peer(dx, dy):
        return dev(zh, (y + dy) % 8, core, x_mirror if dx else x, zl)

    def remote(src, dst, send, recv, device):
        return pltpu.make_async_remote_copy(
            src_ref=src, dst_ref=dst, send_sem=send, recv_sem=recv,
            device_id=device, device_id_type=MESH,
        )

    load_a = pltpu.make_async_copy(a_hbm, a_v, load_sem.at[0])
    load_b = pltpu.make_async_copy(b_hbm, b_v, load_sem.at[1])
    load_w = pltpu.make_async_copy(w_hbm, w_v, load_sem.at[2])
    load_a.start()
    load_b.start()
    load_w.start()

    barrier = pltpu.get_barrier_semaphore()
    greeted = [sibling]
    greeted += [rs_peer(dy, dzh) for dy in range(8) for dzh in range(4) if dy or dzh]
    greeted += [ag_peer(dx, dz) for dx in range(2) for dz in range(8) if dx or dz % 2]
    greeted += [out_peer(1, dy) for dy in range(8)]
    for device in greeted:
        pl.semaphore_signal(barrier, inc=1, device_id=device, device_id_type=MESH)

    load_a.wait()
    load_b.wait()
    load_w.wait()
    out_ref[...] = nn(a_v[...], w_v[...]).astype(BF16)
    pl.semaphore_wait(barrier, len(greeted))

    def columns(dy, half):
        return pl.ds(pl.multiple_of((y + dy) % 8 * BLOCK + half * HALF, HALF), HALF)

    swap_b = remote(b_v, b_s, bs_send, bs_recv, sibling)
    swap_b.start()
    swaps = {}
    for dy in Y_ORDER:
        swaps[dy] = remote(
            a_v.at[:, columns(dy, 1 - core)], a_s.at[dy], as_send.at[dy], as_recv.at[dy], sibling
        )
        swaps[dy].start()
    swap_b.wait()
    b_t = jnp.concatenate([b_v[...], b_s[...]], axis=0).astype(F32).T.astype(BF16)
    for dy in Y_ORDER:
        swaps[dy].wait()
        a_both = jnp.concatenate([a_v[:, columns(dy, core)], a_s[dy]], axis=0)
        part[dy] = nn(b_t, a_both).astype(BF16)
        for dzh in (2, 1, 3, 0):
            if dy or dzh:
                rows = pl.ds(pl.multiple_of((zh + dzh) % 4 * 32, 32), 32)
                remote(
                    part.at[dy, rows], rs_buf.at[dy * 4 + dzh], rs_send, rs_recv, rs_peer(dy, dzh)
                ).start()

    all_rs = rs_buf.at[pl.ds(1, 31)]
    remote(all_rs, all_rs, rs_send, rs_recv, sibling).wait_recv()
    total = part[0, pl.ds(pl.multiple_of(zh * 32, 32), 32), :].astype(F32)
    for slot in range(1, 32):
        total += rs_buf[slot].astype(F32)
    own_rows = pl.ds(pl.multiple_of((x % 2 * 2 + zl) * 128 + zh * 32, 32), 32)
    tile[core, own_rows, :] = total.astype(BF16)

    for dx in (1, 0):
        for dz in (4, 3, 5, 2, 6, 1, 7, 0):
            if dx or dz:
                piece = tile.at[core, own_rows]
                remote(piece, piece, ag_send, ag_recv, ag_peer(dx, dz)).start()
    all_ag = tile.at[core, pl.ds(0, 480)]
    remote(all_ag, all_ag, ag_send, ag_recv, sibling).wait_recv()
    swap_t = remote(tile.at[core], tile.at[core], th_send, th_recv, sibling)
    swap_t.start()
    swap_t.wait()

    @pl.when(core == 0)
    def _():
        u_ref[0:HALF, :] = tile[0].T
        u_ref[HALF:BLOCK, :] = tile[1].T

    @pl.when(core == 1)
    def _():
        u_ref[:, 0:HALF] = tile[0]
        u_ref[:, HALF:BLOCK] = tile[1]

    diagonal = lax.broadcasted_iota(jnp.int32, (BLOCK, BLOCK), 0) == lax.broadcasted_iota(
        jnp.int32, (BLOCK, BLOCK), 1
    )
    t0[...] = nt(u_ref[...], u_ref[...])
    trace = jnp.sum(jnp.where(diagonal, t0[...], 0.0), keepdims=True)
    shift = DAMPING * trace / BLOCK
    m0[...] = t0[...] + jnp.where(diagonal, shift, 0.0)
    norm = jnp.sqrt(jnp.sum(m0[...] * m0[...], keepdims=True))
    m0[...] = m0[...] * (1.0 / norm)
    b0[...] = m0[...].astype(BF16)

    def newton(m, m_half, m_next):
        e = (nn(m_half[...], m_half[...]) * 0.0625 - 0.625 * m[...]).astype(BF16)
        b1[...] = e
        t0[...] = 1.5625 * m[...] + nn(b1[...], m_half[...])
        xr[...] = t0[...].astype(BF16)
        m_next[...] = 1.5625 * t0[...] + nn(b1[...], xr[...])

    newton(m0, b0, m1)
    u1 = m1[...].astype(BF16)
    m0[...] = nn(b0[...], u1) * 0.0625 - 0.3125 * (m0[...] + m1[...])
    b0[...] = u1
    newton(m1, b0, m2)
    b0[...] = m0[...].astype(BF16)
    b1[...] = m2[...].astype(BF16)
    root = 1.25 * m0[...] - 0.390625 * m2[...] - 0.25 * nn(b0[...], b1[...])
    root = root + jnp.where(diagonal, 1.953125, 0.0)
    xr[...] = (root * lax.rsqrt(jnp.sqrt(norm))).astype(BF16)

    give_half = remote(hbuf, hbuf, ex_send, ex_recv, sibling)
    give_root = remote(xr.at[:, pl.ds(0, HALF)], rbuf, ex_send, ex_recv, sibling)

    @pl.when(core == 0)
    def _():
        for slot, x_ in ((0, x), (1, x_mirror)):
            rows = pl.ds(pl.multiple_of((x_ * 2 + zl) * 64, 64), 64)
            hbuf[slot * 64 : slot * 64 + 64, :] = nn(xr[rows, :], u_ref[...]).astype(BF16)
        give_half.start()
        give_half.wait_send()
        give_root.wait_recv()

    @pl.when(core == 1)
    def _():
        give_root.start()
        rbuf[...] = xr[:, HALF:BLOCK]
        give_root.wait_send()
        give_half.wait_recv()

    piece = (nn(hbuf[...], rbuf[...]) * math.sqrt(BLOCK)).astype(BF16)
    osrc[0] = piece[0:64]
    osrc[1] = piece[64:128]
    place = c * 8 + y
    for dy in Y_ORDER:
        for dx in (1, 0):
            if dx or dy:
                remote(
                    osrc.at[dx], oland.at[core, place], o_send, o_recv, out_peer(dx, dy)
                ).start()
    oland[core, place] = osrc[0]
    all_out = oland.at[core, pl.ds(0, 15)]
    remote(all_out, all_out, o_send, o_recv, sibling).wait_recv()
    swap_o = remote(oland.at[core], oland.at[core], of_send, of_recv, sibling)
    swap_o.start()

    def finish(half, cb):
        return pltpu.make_async_copy(
            oland.at[half, pl.ds(cb * 8, 8)],
            upd_hbm.at[:, :, pl.ds(pl.multiple_of(cb * BLOCK + half * HALF, HALF), HALF)],
            fin_sem.at[half, cb],
        )

    finish(core, 0).start()
    finish(core, 1).start()
    swap_o.wait()
    finish(1 - core, 0).start()
    finish(1 - core, 1).start()

    remote(all_rs, all_rs, rs_send, rs_recv, sibling).wait_send()
    remote(all_ag, all_ag, ag_send, ag_recv, sibling).wait_send()
    remote(all_out, all_out, o_send, o_recv, sibling).wait_send()
    for half in range(2):
        for cb in range(2):
            finish(half, cb).wait()


def on_device(inputs, weight, cotangent):
    anywhere = pl.BlockSpec(memory_space=pl.ANY)
    square = (BLOCK, BLOCK)
    dma = pltpu.SemaphoreType.DMA
    return pl.pallas_call(
        kernel,
        out_shape=(
            jax.ShapeDtypeStruct((128, 128), BF16),
            jax.ShapeDtypeStruct((8, 64, CB * BLOCK), BF16),
        ),
        in_specs=[anywhere] * 3,
        out_specs=(pl.BlockSpec(memory_space=pltpu.VMEM), anywhere),
        scratch_shapes=[
            pltpu.VMEM((128, D), BF16),
            pltpu.VMEM((D, 128), BF16),
            pltpu.VMEM((128, 128), BF16),
            pltpu.VMEM((8, 128, HALF), BF16),
            pltpu.VMEM((128, 128), BF16),
            pltpu.VMEM((8, 128, HALF), BF16),
            pltpu.VMEM((32, 32, HALF), BF16),
            pltpu.VMEM((2, BLOCK, HALF), BF16),
            pltpu.VMEM(square, BF16),
            pltpu.VMEM(square, F32),
            pltpu.VMEM(square, F32),
            pltpu.VMEM(square, F32),
            pltpu.VMEM(square, F32),
            pltpu.VMEM(square, BF16),
            pltpu.VMEM(square, BF16),
            pltpu.VMEM(square, BF16),
            pltpu.VMEM((128, BLOCK), BF16),
            pltpu.VMEM((BLOCK, HALF), BF16),
            pltpu.VMEM((2, 64, HALF), BF16),
            pltpu.VMEM((2, 16, 64, HALF), BF16),
            dma((3,)),
            dma((8,)), dma((8,)),
            dma, dma,
            dma, dma,
            dma, dma,
            dma, dma,
            dma, dma,
            dma, dma,
            dma, dma,
            dma((2, 2)),
        ],
        compiler_params=pltpu.CompilerParams(
            collective_id=0, has_side_effects=True, vmem_limit_bytes=48 * 2**20
        ),
    )(inputs, weight, cotangent)


def solution(mesh):
    placed = (P("dp", None), P(None, "pre"), P("dp", "pre"))
    return jax.shard_map(
        on_device,
        mesh=mesh,
        in_specs=placed,
        out_specs=(P("dp", "pre"), P(None, "pre", None)),
        check_vma=False,
    )
```

```python
import math

import jax
import jax.numpy as jnp
from jax import lax
from jax.experimental import pallas as pl
from jax.experimental.pallas import tpu as pltpu
from jax.sharding import PartitionSpec as P

D = 4096
BLOCK = 512
CB = 2
HALF = BLOCK // 2
DAMPING = 0.1
MESH = pl.DeviceIdType.MESH
BF16 = jnp.bfloat16
F32 = jnp.float32

Y_ORDER = (4, 3, 5, 2, 6, 1, 7, 0)


def nn(a, b):
    return lax.dot_general(a, b, (((1,), (0,)), ((), ())), preferred_element_type=F32)


def nt(a, b):
    return lax.dot_general(a, b, (((1,), (1,)), ((), ())), preferred_element_type=F32)


def kernel(
    a_hbm, w_hbm, b_hbm, out_ref, upd_ref,
    a_v, w_v, b_v, a_s, b_s, part, rs_buf, tile, u_ref,
    m0, m1, m2, t0, b0, b1, xr, hbuf, rbuf, osrc,
    load_sem, as_send, as_recv, bs_send, bs_recv, rs_send, rs_recv,
    ag_send, ag_recv, th_send, th_recv, ex_send, ex_recv,
    o_send, o_recv, of_send, of_recv,
):
    dp = lax.axis_index("dp")
    pre = lax.axis_index("pre")
    zh, y, core = dp // 16, (dp // 2) % 8, dp % 2
    x, zl = pre // 2, pre % 2
    z = zh * 2 + zl
    c = x // 2
    x_pair = c * 2 + (1 - x % 2)
    x_mirror = 3 - x

    def dev(zh_, y_, core_, x_, zl_):
        return ((zh_ * 8 + y_) * 2 + core_, x_ * 2 + zl_)

    sibling = dev(zh, y, 1 - core, x, zl)

    def rs_peer(dy, dzh):
        return dev((zh + dzh) % 4, (y + dy) % 8, core, x, zl)

    def ag_peer(dx, dz):
        z_ = (z + dz) % 8
        return dev(z_ // 2, y, core, x_pair if dx else x, z_ % 2)

    def out_peer(dx, dy):
        return dev(zh, (y + dy) % 8, core, x_mirror if dx else x, zl)

    def remote(src, dst, send, recv, device):
        return pltpu.make_async_remote_copy(
            src_ref=src, dst_ref=dst, send_sem=send, recv_sem=recv,
            device_id=device, device_id_type=MESH,
        )

    load_a = pltpu.make_async_copy(a_hbm, a_v, load_sem.at[0])
    load_b = pltpu.make_async_copy(b_hbm, b_v, load_sem.at[1])
    load_w = pltpu.make_async_copy(w_hbm, w_v, load_sem.at[2])
    load_a.start()
    load_b.start()
    load_w.start()

    barrier = pltpu.get_barrier_semaphore()
    greeted = [sibling]
    greeted += [rs_peer(dy, dzh) for dy in range(8) for dzh in range(4) if dy or dzh]
    greeted += [ag_peer(dx, dz) for dx in range(2) for dz in range(8) if dx or dz % 2]
    greeted += [out_peer(1, dy) for dy in range(8)]
    for device in greeted:
        pl.semaphore_signal(barrier, inc=1, device_id=device, device_id_type=MESH)

    load_a.wait()
    load_b.wait()
    pl.semaphore_wait(barrier, len(greeted))

    def columns(dy, half):
        return pl.ds(pl.multiple_of((y + dy) % 8 * BLOCK + half * HALF, HALF), HALF)

    swap_b = remote(b_v, b_s, bs_send, bs_recv, sibling)
    swap_b.start()
    swaps = {}
    for dy in Y_ORDER:
        swaps[dy] = remote(
            a_v.at[:, columns(dy, 1 - core)], a_s.at[dy], as_send.at[dy], as_recv.at[dy], sibling
        )
        swaps[dy].start()
    swap_b.wait()
    b_t = jnp.concatenate([b_v[...], b_s[...]], axis=0).astype(F32).T.astype(BF16)
    for dy in Y_ORDER:
        swaps[dy].wait()
        a_both = jnp.concatenate([a_v[:, columns(dy, core)], a_s[dy]], axis=0)
        part[dy] = nn(b_t, a_both).astype(BF16)
        for dzh in (2, 1, 3, 0):
            if dy or dzh:
                rows = pl.ds(pl.multiple_of((zh + dzh) % 4 * 32, 32), 32)
                remote(
                    part.at[dy, rows], rs_buf.at[dy * 4 + dzh], rs_send, rs_recv, rs_peer(dy, dzh)
                ).start()

    load_w.wait()
    out_ref[...] = nn(a_v[...], w_v[...]).astype(BF16)

    all_rs = rs_buf.at[pl.ds(1, 31)]
    remote(all_rs, all_rs, rs_send, rs_recv, sibling).wait_recv()
    total = part[0, pl.ds(pl.multiple_of(zh * 32, 32), 32), :].astype(F32)
    for slot in range(1, 32):
        total += rs_buf[slot].astype(F32)
    own_rows = pl.ds(pl.multiple_of((x % 2 * 2 + zl) * 128 + zh * 32, 32), 32)
    tile[core, own_rows, :] = total.astype(BF16)

    for dx in (1, 0):
        for dz in (4, 3, 5, 2, 6, 1, 7, 0):
            if dx or dz:
                piece = tile.at[core, own_rows]
                remote(piece, piece, ag_send, ag_recv, ag_peer(dx, dz)).start()
    all_ag = tile.at[core, pl.ds(0, 480)]
    remote(all_ag, all_ag, ag_send, ag_recv, sibling).wait_recv()
    swap_t = remote(tile.at[core], tile.at[core], th_send, th_recv, sibling)
    swap_t.start()
    swap_t.wait()

    @pl.when(core == 0)
    def _():
        u_ref[0:HALF, :] = tile[0].T
        u_ref[HALF:BLOCK, :] = tile[1].T

    @pl.when(core == 1)
    def _():
        u_ref[:, 0:HALF] = tile[0]
        u_ref[:, HALF:BLOCK] = tile[1]

    diagonal = lax.broadcasted_iota(jnp.int32, (BLOCK, BLOCK), 0) == lax.broadcasted_iota(
        jnp.int32, (BLOCK, BLOCK), 1
    )
    t0[...] = nt(u_ref[...], u_ref[...])
    trace = jnp.sum(jnp.where(diagonal, t0[...], 0.0), keepdims=True)
    shift = DAMPING * trace / BLOCK
    m0[...] = t0[...] + jnp.where(diagonal, shift, 0.0)
    norm = jnp.sqrt(jnp.sum(m0[...] * m0[...], keepdims=True))
    m0[...] = m0[...] * (1.0 / norm)
    b0[...] = m0[...].astype(BF16)

    def newton(m, m_half, m_next):
        e = (nn(m_half[...], m_half[...]) * 0.0625 - 0.625 * m[...]).astype(BF16)
        b1[...] = e
        t0[...] = 1.5625 * m[...] + nn(b1[...], m_half[...])
        xr[...] = t0[...].astype(BF16)
        m_next[...] = 1.5625 * t0[...] + nn(b1[...], xr[...])

    newton(m0, b0, m1)
    u1 = m1[...].astype(BF16)
    m0[...] = nn(b0[...], u1) * 0.0625 - 0.3125 * (m0[...] + m1[...])
    b0[...] = u1
    newton(m1, b0, m2)
    b0[...] = m0[...].astype(BF16)
    b1[...] = m2[...].astype(BF16)
    root = 1.25 * m0[...] - 0.390625 * m2[...] - 0.25 * nn(b0[...], b1[...])
    root = root + jnp.where(diagonal, 1.953125, 0.0)
    xr[...] = (root * lax.rsqrt(jnp.sqrt(norm))).astype(BF16)

    give_half = remote(hbuf, hbuf, ex_send, ex_recv, sibling)
    give_root = remote(xr.at[:, pl.ds(0, HALF)], rbuf, ex_send, ex_recv, sibling)

    @pl.when(core == 0)
    def _():
        for slot, x_ in ((0, x), (1, x_mirror)):
            rows = pl.ds(pl.multiple_of((x_ * 2 + zl) * 64, 64), 64)
            hbuf[slot * 64 : slot * 64 + 64, :] = nn(xr[rows, :], u_ref[...]).astype(BF16)
        give_half.start()
        give_half.wait_send()
        give_root.wait_recv()

    @pl.when(core == 1)
    def _():
        give_root.start()
        rbuf[...] = xr[:, HALF:BLOCK]
        give_root.wait_send()
        give_half.wait_recv()

    def place(row_block, cb):
        lanes = pl.ds(pl.multiple_of(cb * BLOCK + core * HALF, HALF), HALF)
        return upd_ref.at[row_block, :, lanes]

    def landing(dx, dy):
        return place((y + 8 - dy) % 8, 1 - c if dx else c)

    def give(dx, dy):
        remote(osrc.at[dx], place(y, c), o_send, o_recv.at[dx, dy], out_peer(dx, dy)).start()

    def take(dx, dy):
        landed = landing(dx, dy)
        remote(landed, landed, o_send, o_recv.at[dx, dy], sibling).wait_recv()
        remote(landed, landed, of_send, of_recv, sibling).start()

    def hand_on(dx, dy, step):
        landed = landing(dx, dy)
        remote(
            landed, landed, o_send, o_recv.at[dx, (dy + step) % 8], out_peer(0, step % 8)
        ).start()

    piece = (nn(hbuf[...], rbuf[...]) * math.sqrt(BLOCK)).astype(BF16)
    osrc[0] = piece[0:64]
    osrc[1] = piece[64:128]
    for dx, dy in ((1, 2), (1, 6), (0, 2), (0, 6), (1, 1), (1, 7), (0, 1), (0, 7), (1, 0)):
        give(dx, dy)
    remote(osrc.at[0], place(y, c), of_send, of_recv, sibling).start()
    place(y, c)[...] = osrc[0]
    for dx, dy, step in ((0, 2, 1), (0, 6, -1), (1, 2, 1), (1, 6, -1)):
        take(dx, dy)
        if dx == (dy == 6):
            hand_on(dx, dy, 2 * step)
        hand_on(dx, dy, step)
    for dx, dy in ((1, 0), (0, 1), (0, 7), (1, 1), (1, 7), (0, 3), (0, 5), (0, 4), (1, 3), (1, 5), (1, 4)):
        take(dx, dy)
    all_half = upd_ref.at[pl.ds(0, 4)]
    remote(all_half, all_half, of_send, of_recv, sibling).wait()

    all_out = tile.at[0, pl.ds(0, 480)]
    remote(all_rs, all_rs, rs_send, rs_recv, sibling).wait_send()
    remote(all_ag, all_ag, ag_send, ag_recv, sibling).wait_send()
    remote(all_out, all_out, o_send, th_recv, sibling).wait_send()
    remote(all_out, all_out, o_send, th_recv, sibling).wait_send()


def on_device(inputs, weight, cotangent):
    square = (BLOCK, BLOCK)
    dma = pltpu.SemaphoreType.DMA
    return pl.pallas_call(
        kernel,
        out_shape=(
            jax.ShapeDtypeStruct((128, 128), BF16),
            jax.ShapeDtypeStruct((8, 64, CB * BLOCK), BF16),
        ),
        in_specs=[pl.BlockSpec(memory_space=pltpu.HBM)] * 3,
        out_specs=(pl.BlockSpec(memory_space=pltpu.VMEM),) * 2,
        scratch_shapes=[
            pltpu.VMEM((128, D), BF16),
            pltpu.VMEM((D, 128), BF16),
            pltpu.VMEM((128, 128), BF16),
            pltpu.VMEM((8, 128, HALF), BF16),
            pltpu.VMEM((128, 128), BF16),
            pltpu.VMEM((8, 128, HALF), BF16),
            pltpu.VMEM((32, 32, HALF), BF16),
            pltpu.VMEM((2, BLOCK, HALF), BF16),
            pltpu.VMEM(square, BF16),
            pltpu.VMEM(square, F32),
            pltpu.VMEM(square, F32),
            pltpu.VMEM(square, F32),
            pltpu.VMEM(square, F32),
            pltpu.VMEM(square, BF16),
            pltpu.VMEM(square, BF16),
            pltpu.VMEM(square, BF16),
            pltpu.VMEM((128, BLOCK), BF16),
            pltpu.VMEM((BLOCK, HALF), BF16),
            pltpu.VMEM((2, 64, HALF), BF16),
            dma((3,)),
            dma((8,)), dma((8,)),
            dma, dma,
            dma, dma,
            dma, dma,
            dma, dma,
            dma, dma,
            dma, dma((2, 8)),
            dma, dma,
        ],
        compiler_params=pltpu.CompilerParams(
            collective_id=0, has_side_effects=True, vmem_limit_bytes=48 * 2**20
        ),
    )(*(pltpu.with_memory_space_constraint(v, pltpu.HBM) for v in (inputs, weight, cotangent)))


def solution(mesh):
    placed = (P("dp", None), P(None, "pre"), P("dp", "pre"))
    return jax.shard_map(
        on_device,
        mesh=mesh,
        in_specs=placed,
        out_specs=(P("dp", "pre"), P(None, "pre", None)),
        check_vma=False,
    )
```

```python
import math

import jax
import jax.numpy as jnp
from jax import lax
from jax.experimental import pallas as pl
from jax.experimental.pallas import tpu as pltpu
from jax.sharding import PartitionSpec as P

D = 4096
BLOCK = 512
CB = 2
HALF = BLOCK // 2
DAMPING = 0.1
MESH = pl.DeviceIdType.MESH
BF16 = jnp.bfloat16
F32 = jnp.float32

Y_ORDER = (4, 3, 5, 2, 6, 1, 7, 0)


def nn(a, b):
    return lax.dot_general(a, b, (((1,), (0,)), ((), ())), preferred_element_type=F32)


def nt(a, b):
    return lax.dot_general(a, b, (((1,), (1,)), ((), ())), preferred_element_type=F32)


def kernel(
    a_hbm, w_hbm, b_hbm, out_ref, upd_ref,
    a_v, w_v, b_v, a_s, b_s, part, y1, z1, zs, z2, y2, tile, u_ref,
    m0, m1, m2, t0, b0, b1, xr, hbuf, rbuf, osrc,
    load_sem, as_send, as_recv, bs_send, bs_recv,
    y1_send, y1_recv, z1_send, z1_recv, z2_send, z2_recv, y2_send, y2_recv,
    yg_send, yg_recv, zg_send, zg_recv, th_send, th_recv, ex_send, ex_recv,
    o_send, o_recv, of_send, of_recv,
):
    dp = lax.axis_index("dp")
    pre = lax.axis_index("pre")
    zh, y, core = dp // 16, (dp // 2) % 8, dp % 2
    x, zl = pre // 2, pre % 2
    z = zh * 2 + zl
    c = x // 2
    x_pair = c * 2 + (1 - x % 2)
    x_mirror = 3 - x

    def dev(zh_, y_, core_, x_, zl_):
        return ((zh_ * 8 + y_) * 2 + core_, x_ * 2 + zl_)

    sibling = dev(zh, y, 1 - core, x, zl)

    def y_peer(dy):
        return dev(zh, (y + dy) % 8, core, x, zl)

    def z_peer(dzh):
        return dev((zh + dzh) % 4, y, core, x, zl)

    def ag_peer(dx, dz):
        z_ = (z + dz) % 8
        return dev(z_ // 2, y, core, x_pair if dx else x, z_ % 2)

    def out_peer(dx, dy):
        return dev(zh, (y + dy) % 8, core, x_mirror if dx else x, zl)

    def remote(src, dst, send, recv, device):
        return pltpu.make_async_remote_copy(
            src_ref=src, dst_ref=dst, send_sem=send, recv_sem=recv,
            device_id=device, device_id_type=MESH,
        )

    load_a = pltpu.make_async_copy(a_hbm, a_v, load_sem.at[0])
    load_b = pltpu.make_async_copy(b_hbm, b_v, load_sem.at[1])
    load_w = pltpu.make_async_copy(w_hbm, w_v, load_sem.at[2])
    load_a.start()
    load_b.start()
    load_w.start()

    barrier = pltpu.get_barrier_semaphore()
    greeted = [sibling]
    greeted += [y_peer(dy) for dy in range(1, 8)]
    greeted += [ag_peer(dx, dz) for dx in range(2) for dz in range(8) if dx or dz]
    greeted += [out_peer(1, dy) for dy in range(8)]
    for device in greeted:
        pl.semaphore_signal(barrier, inc=1, device_id=device, device_id_type=MESH)

    load_a.wait()
    load_b.wait()
    pl.semaphore_wait(barrier, len(greeted))

    def columns(dy, half):
        return pl.ds(pl.multiple_of((y + dy) % 8 * BLOCK + half * HALF, HALF), HALF)

    swap_b = remote(b_v, b_s, bs_send, bs_recv, sibling)
    swap_b.start()
    swaps = {}
    for dy in Y_ORDER:
        swaps[dy] = remote(
            a_v.at[:, columns(dy, 1 - core)], a_s.at[dy], as_send.at[dy], as_recv.at[dy], sibling
        )
        swaps[dy].start()
    swap_b.wait()
    b_t = jnp.concatenate([b_v[...], b_s[...]], axis=0).astype(F32).T.astype(BF16)
    b_t = jnp.concatenate(
        [b_t[h * 32 + path * 16 : h * 32 + path * 16 + 16] for path in range(2) for h in range(4)],
        axis=0,
    )
    for i, dy in enumerate(Y_ORDER):
        swaps[dy].wait()
        a_both = jnp.concatenate([a_v[:, columns(dy, core)], a_s[dy]], axis=0)
        part[i] = nn(b_t, a_both).astype(BF16).reshape(2, 4, 16, HALF)
        if dy:
            remote(part.at[i, 0], y1.at[i], y1_send, y1_recv, y_peer(dy)).start()
        if i % 4 == 3:
            some = pl.ds(i - 3, 4)
            for dzh in (2, 1, 3):
                remote(
                    part.at[some, 1, (zh + dzh) % 4], z1.at[dzh - 1, some],
                    z1_send, z1_recv, z_peer(dzh),
                ).start()

    load_w.wait()
    out_ref[...] = nn(a_v[...], w_v[...]).astype(BF16)

    remote(z1, z1, z1_send, z1_recv, sibling).wait_recv()
    for i, dy in enumerate(Y_ORDER):
        terms = part[i, 1, zh].astype(F32)
        for dzh in range(3):
            terms += z1[dzh, i].astype(F32)
        zs[i] = terms.astype(BF16)
        if dy:
            remote(zs.at[i], z2.at[i], z2_send, z2_recv, y_peer(dy)).start()
    remote(y1, y1, y1_send, y1_recv, sibling).wait_recv()
    total = part[7, 0].astype(F32)
    for i in range(7):
        total += y1[i].astype(F32)
    y2[zh] = total.astype(BF16)
    for dzh in (2, 1, 3):
        remote(y2.at[zh], y2.at[zh], y2_send, y2_recv, z_peer(dzh)).start()

    mine = x % 2 * 2 + zl
    all_z2 = z2.at[pl.ds(0, 7)]
    remote(all_z2, all_z2, z2_send, z2_recv, sibling).wait_recv()
    total = zs[7].astype(F32)
    for i in range(7):
        total += z2[i].astype(F32)
    tile[core, mine, zh, 1] = total.astype(BF16)
    piece = tile.at[core, mine, zh, 1]
    for dx in (1, 0):
        for dz in (4, 3, 5, 2, 6, 1, 7, 0):
            if dx or dz:
                remote(piece, piece, zg_send, zg_recv, ag_peer(dx, dz)).start()
    three = y2.at[pl.ds(0, 3)]
    remote(three, three, y2_send, y2_recv, sibling).wait_recv()
    total = y2[0].astype(F32)
    for h in range(1, 4):
        total += y2[h].astype(F32)
    tile[core, mine, :, 0] = total.astype(BF16)
    piece = tile.at[core, mine, :, 0]
    for x_, zl_ in ((x_pair, 1 - zl), (x_pair, zl), (x, 1 - zl)):
        remote(piece, piece, yg_send, yg_recv, dev(zh, y, core, x_, zl_)).start()
    remote(three, three, yg_send, yg_recv, sibling).wait_recv()
    swap_y = remote(
        tile.at[core, :, :, 0], tile.at[core, :, :, 0], th_send.at[0], th_recv.at[0], sibling
    )
    swap_y.start()
    all_zg = z1.at[:, pl.ds(0, 5)]
    remote(all_zg, all_zg, zg_send, zg_recv, sibling).wait_recv()
    swap_z = remote(
        tile.at[core, :, :, 1], tile.at[core, :, :, 1], th_send.at[1], th_recv.at[1], sibling
    )
    swap_z.start()
    swap_y.wait()
    swap_z.wait()

    @pl.when(core == 0)
    def _():
        u_ref[0:HALF, :] = tile[0].reshape(BLOCK, HALF).T
        u_ref[HALF:BLOCK, :] = tile[1].reshape(BLOCK, HALF).T

    @pl.when(core == 1)
    def _():
        u_ref[:, 0:HALF] = tile[0].reshape(BLOCK, HALF)
        u_ref[:, HALF:BLOCK] = tile[1].reshape(BLOCK, HALF)

    diagonal = lax.broadcasted_iota(jnp.int32, (BLOCK, BLOCK), 0) == lax.broadcasted_iota(
        jnp.int32, (BLOCK, BLOCK), 1
    )
    t0[...] = nt(u_ref[...], u_ref[...])
    trace = jnp.sum(jnp.where(diagonal, t0[...], 0.0), keepdims=True)
    shift = DAMPING * trace / BLOCK
    m0[...] = t0[...] + jnp.where(diagonal, shift, 0.0)
    norm = jnp.sqrt(jnp.sum(m0[...] * m0[...], keepdims=True))
    m0[...] = m0[...] * (1.0 / norm)
    b0[...] = m0[...].astype(BF16)

    def newton(m, m_half, m_next):
        e = (nn(m_half[...], m_half[...]) * 0.0625 - 0.625 * m[...]).astype(BF16)
        b1[...] = e
        t0[...] = 1.5625 * m[...] + nn(b1[...], m_half[...])
        xr[...] = t0[...].astype(BF16)
        m_next[...] = 1.5625 * t0[...] + nn(b1[...], xr[...])

    newton(m0, b0, m1)
    u1 = m1[...].astype(BF16)
    m0[...] = nn(b0[...], u1) * 0.0625 - 0.3125 * (m0[...] + m1[...])
    b0[...] = u1
    newton(m1, b0, m2)
    b0[...] = m0[...].astype(BF16)
    b1[...] = m2[...].astype(BF16)
    root = 1.25 * m0[...] - 0.390625 * m2[...] - 0.25 * nn(b0[...], b1[...])
    root = root + jnp.where(diagonal, 1.953125, 0.0)
    xr[...] = (root * lax.rsqrt(jnp.sqrt(norm))).astype(BF16)

    give_half = remote(hbuf, hbuf, ex_send, ex_recv, sibling)
    give_root = remote(xr.at[:, pl.ds(0, HALF)], rbuf, ex_send, ex_recv, sibling)

    @pl.when(core == 0)
    def _():
        for slot, x_ in ((0, x), (1, x_mirror)):
            rows = pl.ds(pl.multiple_of((x_ * 2 + zl) * 64, 64), 64)
            hbuf[slot * 64 : slot * 64 + 64, :] = nn(xr[rows, :], u_ref[...]).astype(BF16)
        give_half.start()
        give_half.wait_send()
        give_root.wait_recv()

    @pl.when(core == 1)
    def _():
        give_root.start()
        rbuf[...] = xr[:, HALF:BLOCK]
        give_root.wait_send()
        give_half.wait_recv()

    def place(row_block, cb):
        lanes = pl.ds(pl.multiple_of(cb * BLOCK + core * HALF, HALF), HALF)
        return upd_ref.at[row_block, :, lanes]

    def landing(dx, dy):
        return place((y + 8 - dy) % 8, 1 - c if dx else c)

    def give(dx, dy):
        remote(osrc.at[dx], place(y, c), o_send, o_recv.at[dx, dy], out_peer(dx, dy)).start()

    def take(dx, dy):
        landed = landing(dx, dy)
        remote(landed, landed, o_send, o_recv.at[dx, dy], sibling).wait_recv()
        remote(landed, landed, of_send, of_recv, sibling).start()

    def hand_on(dx, dy, step):
        landed = landing(dx, dy)
        remote(
            landed, landed, o_send, o_recv.at[dx, (dy + step) % 8], out_peer(0, step % 8)
        ).start()

    piece = (nn(hbuf[...], rbuf[...]) * math.sqrt(BLOCK)).astype(BF16)
    osrc[0] = piece[0:64]
    osrc[1] = piece[64:128]
    for dx, dy in ((1, 2), (1, 6), (0, 2), (0, 6), (1, 1), (1, 7), (0, 1), (0, 7), (1, 0)):
        give(dx, dy)
    remote(osrc.at[0], place(y, c), of_send, of_recv, sibling).start()
    place(y, c)[...] = osrc[0]
    for dx, dy, step in ((0, 2, 1), (0, 6, -1), (1, 2, 1), (1, 6, -1)):
        take(dx, dy)
        if dx == (dy == 6):
            hand_on(dx, dy, 2 * step)
        hand_on(dx, dy, step)
    for dx, dy in ((1, 0), (0, 1), (0, 7), (1, 1), (1, 7), (0, 3), (0, 5), (0, 4), (1, 3), (1, 5), (1, 4)):
        take(dx, dy)
    all_half = upd_ref.at[pl.ds(0, 4)]
    remote(all_half, all_half, of_send, of_recv, sibling).wait()

    remote(y1, y1, y1_send, y1_recv, sibling).wait_send()
    remote(z1, z1, z1_send, z1_recv, sibling).wait_send()
    remote(all_z2, all_z2, z2_send, z2_recv, sibling).wait_send()
    remote(three, three, y2_send, y2_recv, sibling).wait_send()
    remote(three, three, yg_send, yg_recv, sibling).wait_send()
    remote(all_zg, all_zg, zg_send, zg_recv, sibling).wait_send()
    all_out = tile.at[0, pl.ds(0, 3)]
    for _ in range(2):
        remote(all_out, all_out, o_send, y2_recv, sibling).wait_send()
    remote(three, three, o_send, y2_recv, sibling).wait_send()


def on_device(inputs, weight, cotangent):
    square = (BLOCK, BLOCK)
    dma = pltpu.SemaphoreType.DMA
    return pl.pallas_call(
        kernel,
        out_shape=(
            jax.ShapeDtypeStruct((128, 128), BF16),
            jax.ShapeDtypeStruct((8, 64, CB * BLOCK), BF16),
        ),
        in_specs=[pl.BlockSpec(memory_space=pltpu.HBM)] * 3,
        out_specs=(pl.BlockSpec(memory_space=pltpu.VMEM),) * 2,
        scratch_shapes=[
            pltpu.VMEM((128, D), BF16),
            pltpu.VMEM((D, 128), BF16),
            pltpu.VMEM((128, 128), BF16),
            pltpu.VMEM((8, 128, HALF), BF16),
            pltpu.VMEM((128, 128), BF16),
            pltpu.VMEM((8, 2, 4, 16, HALF), BF16),
            pltpu.VMEM((7, 4, 16, HALF), BF16),
            pltpu.VMEM((3, 8, 16, HALF), BF16),
            pltpu.VMEM((8, 16, HALF), BF16),
            pltpu.VMEM((8, 16, HALF), BF16),
            pltpu.VMEM((4, 4, 16, HALF), BF16),
            pltpu.VMEM((2, 4, 4, 2, 16, HALF), BF16),
            pltpu.VMEM(square, BF16),
            pltpu.VMEM(square, F32),
            pltpu.VMEM(square, F32),
            pltpu.VMEM(square, F32),
            pltpu.VMEM(square, F32),
            pltpu.VMEM(square, BF16),
            pltpu.VMEM(square, BF16),
            pltpu.VMEM(square, BF16),
            pltpu.VMEM((128, BLOCK), BF16),
            pltpu.VMEM((BLOCK, HALF), BF16),
            pltpu.VMEM((2, 64, HALF), BF16),
            dma((3,)),
            dma((8,)), dma((8,)), dma, dma,
            dma, dma, dma, dma, dma, dma, dma, dma,
            dma, dma, dma, dma, dma((2,)), dma((2,)), dma, dma,
            dma, dma((2, 8)), dma, dma,
        ],
        compiler_params=pltpu.CompilerParams(
            collective_id=0, has_side_effects=True, vmem_limit_bytes=48 * 2**20
        ),
    )(*(pltpu.with_memory_space_constraint(v, pltpu.HBM) for v in (inputs, weight, cotangent)))


def solution(mesh):
    placed = (P("dp", None), P(None, "pre"), P("dp", "pre"))
    return jax.shard_map(
        on_device,
        mesh=mesh,
        in_specs=placed,
        out_specs=(P("dp", "pre"), P(None, "pre", None)),
        check_vma=False,
    )
```

```python
import math

import jax
import jax.numpy as jnp
from jax import lax
from jax.experimental import pallas as pl
from jax.experimental.pallas import tpu as pltpu
from jax.sharding import PartitionSpec as P

D = 4096
BLOCK = 512
CB = 2
HALF = BLOCK // 2
DAMPING = 0.1
MESH = pl.DeviceIdType.MESH
BF16 = jnp.bfloat16
F32 = jnp.float32

Y_ORDER = (4, 3, 5, 2, 6, 1, 7, 0)


def nn(a, b):
    return lax.dot_general(a, b, (((1,), (0,)), ((), ())), preferred_element_type=F32)


def nt(a, b):
    return lax.dot_general(a, b, (((1,), (1,)), ((), ())), preferred_element_type=F32)


def kernel(
    a_hbm, w_hbm, b_hbm, out_ref, upd_ref,
    a_v, w_v, b_v, a_s, b_s, part, part_z, y1, z1, zs, z2, y2, tile, u_ref,
    m0, m1, m2, t0, b0, b1, b2, b3, xr, hbuf, rbuf, osrc,
    load_sem, as_send, as_recv, bs_send, bs_recv,
    y1_send, y1_recv, z1_send, z1_recv, z2_send, z2_recv, y2_send, y2_recv,
    yg_send, yg_recv, zg_send, zg_recv, th_send, th_recv, ex_send, ex_recv,
    o_send, o_recv, of_send, of_recv,
):
    dp = lax.axis_index("dp")
    pre = lax.axis_index("pre")
    zh, y, core = dp // 16, (dp // 2) % 8, dp % 2
    x, zl = pre // 2, pre % 2
    z = zh * 2 + zl
    c = x // 2
    x_pair = c * 2 + (1 - x % 2)
    x_mirror = 3 - x

    def dev(zh_, y_, core_, x_, zl_):
        return ((zh_ * 8 + y_) * 2 + core_, x_ * 2 + zl_)

    sibling = dev(zh, y, 1 - core, x, zl)

    def y_peer(dy):
        return dev(zh, (y + dy) % 8, core, x, zl)

    def z_peer(dzh):
        return dev((zh + dzh) % 4, y, core, x, zl)

    def ag_peer(dx, dz):
        z_ = (z + dz) % 8
        return dev(z_ // 2, y, core, x_pair if dx else x, z_ % 2)

    def out_peer(dx, dy):
        return dev(zh, (y + dy) % 8, core, x_mirror if dx else x, zl)

    def remote(src, dst, send, recv, device):
        return pltpu.make_async_remote_copy(
            src_ref=src, dst_ref=dst, send_sem=send, recv_sem=recv,
            device_id=device, device_id_type=MESH,
        )

    load_a = pltpu.make_async_copy(a_hbm, a_v, load_sem.at[0])
    load_b = pltpu.make_async_copy(b_hbm, b_v, load_sem.at[1])
    load_w = pltpu.make_async_copy(w_hbm, w_v, load_sem.at[2])
    load_a.start()
    load_b.start()
    load_w.start()

    barrier = pltpu.get_barrier_semaphore()
    greeted = [ag_peer(dx, dz) for dz in (4, 3, 5, 2, 6, 1, 7, 0) for dx in (1, 0) if dx or dz]
    greeted += [y_peer(dy) for dy in Y_ORDER if dy]
    greeted += [out_peer(1, dy) for dy in (2, 6, 1, 7, 0)]
    greeted += [sibling]
    for device in greeted:
        pl.semaphore_signal(barrier, inc=1, device_id=device, device_id_type=MESH)

    load_a.wait()
    load_b.wait()
    pl.semaphore_wait(barrier, len(greeted))

    def columns(dy, half):
        return pl.ds(pl.multiple_of((y + dy) % 8 * BLOCK + half * HALF, HALF), HALF)

    swap_b = remote(b_v, b_s, bs_send, bs_recv, sibling)
    swap_b.start()
    swaps = {}
    for dy in Y_ORDER:
        swaps[dy] = remote(
            a_v.at[:, columns(dy, 1 - core)], a_s.at[dy], as_send.at[dy], as_recv.at[dy], sibling
        )
        swaps[dy].start()
    swap_b.wait()
    b_t = jnp.concatenate([b_v[...], b_s[...]], axis=0).astype(F32).T.astype(BF16)
    b_t = jnp.concatenate(
        [b_t[h * 32 + path * 16 : h * 32 + path * 16 + 16] for path in range(2) for h in range(4)],
        axis=0,
    )
    for i, dy in enumerate(Y_ORDER):
        swaps[dy].wait()
        a_both = jnp.concatenate([a_v[:, columns(dy, core)], a_s[dy]], axis=0)
        terms = nn(b_t, a_both).astype(BF16).reshape(2, 4, 16, HALF)
        part[i] = terms[0]
        part_z[:, i] = terms[1]
        if dy:
            remote(part.at[i], y1.at[i], y1_send, y1_recv, y_peer(dy)).start()
        if i % 2:
            some = pl.ds(i - 1, 2)
            for dzh in (1, 3, 2):
                remote(
                    part_z.at[(zh + dzh) % 4, some], z1.at[dzh - 1, some],
                    z1_send, z1_recv, z_peer(dzh),
                ).start()

    load_w.wait()
    out_ref[...] = nn(a_v[...], w_v[...]).astype(BF16)

    remote(z1, z1, z1_send, z1_recv, sibling).wait_recv()
    for i, dy in enumerate(Y_ORDER):
        terms = part_z[zh, i].astype(F32)
        for dzh in range(3):
            terms += z1[dzh, i].astype(F32)
        zs[i] = terms.astype(BF16)
        if dy:
            remote(zs.at[i], z2.at[i], z2_send, z2_recv, y_peer(dy)).start()
    remote(y1, y1, y1_send, y1_recv, sibling).wait_recv()
    total = part[7].astype(F32)
    for i in range(7):
        total += y1[i].astype(F32)
    y2[zh] = total.astype(BF16)
    for dzh in (2, 1, 3):
        remote(y2.at[zh], y2.at[zh], y2_send, y2_recv, z_peer(dzh)).start()

    mine = x % 2 * 2 + zl
    all_z2 = z2.at[pl.ds(0, 7)]
    remote(all_z2, all_z2, z2_send, z2_recv, sibling).wait_recv()
    total = zs[7].astype(F32)
    for i in range(7):
        total += z2[i].astype(F32)
    tile[core, mine, zh, 1] = total.astype(BF16)
    piece = tile.at[core, mine, zh, 1]
    for dx in (1, 0):
        for dz in (4, 3, 5, 2, 6, 1, 7, 0):
            if dx or dz:
                remote(piece, piece, zg_send, zg_recv, ag_peer(dx, dz)).start()
    three = y2.at[pl.ds(0, 3)]
    remote(three, three, y2_send, y2_recv, sibling).wait_recv()
    total = y2[0].astype(F32)
    for h in range(1, 4):
        total += y2[h].astype(F32)
    tile[core, mine, :, 0] = total.astype(BF16)
    piece = tile.at[core, mine, :, 0]
    for x_, zl_ in ((x_pair, 1 - zl), (x_pair, zl), (x, 1 - zl)):
        remote(piece, piece, yg_send, yg_recv, dev(zh, y, core, x_, zl_)).start()
    remote(three, three, yg_send, yg_recv, sibling).wait_recv()
    swap_y = remote(
        tile.at[core, :, :, 0], tile.at[core, :, :, 0], th_send.at[0], th_recv.at[0], sibling
    )
    swap_y.start()
    all_zg = z1.at[:, pl.ds(0, 5)]
    remote(all_zg, all_zg, zg_send, zg_recv, sibling).wait_recv()
    swap_z = remote(
        tile.at[core, :, :, 1], tile.at[core, :, :, 1], th_send.at[1], th_recv.at[1], sibling
    )
    swap_z.start()
    swap_y.wait()
    swap_z.wait()

    @pl.when(core == 0)
    def _():
        u_ref[0:HALF, :] = tile[0].reshape(BLOCK, HALF).T
        u_ref[HALF:BLOCK, :] = tile[1].reshape(BLOCK, HALF).T

    @pl.when(core == 1)
    def _():
        u_ref[:, 0:HALF] = tile[0].reshape(BLOCK, HALF)
        u_ref[:, HALF:BLOCK] = tile[1].reshape(BLOCK, HALF)

    def eye(n):
        return lax.broadcasted_iota(jnp.int32, (n, n), 0) == lax.broadcasted_iota(
            jnp.int32, (n, n), 1
        )

    t0[...] = nt(u_ref[...], u_ref[...])
    blocks = [pl.ds(128 * i, 128) for i in range(4)]
    trace = sum(jnp.where(eye(128), t0[at, at], 0.0) for at in blocks)
    trace = jnp.sum(trace, keepdims=True)
    shift = DAMPING * trace / BLOCK
    energy = jnp.sum(t0[...] * t0[...], keepdims=True)
    norm = jnp.sqrt(energy + 2.0 * shift * trace + BLOCK * shift * shift)
    for at in blocks:
        t0[at, at] = t0[at, at] + jnp.where(eye(128), shift, 0.0)
    scaled = t0[...] * (1.0 / norm)
    m0[...] = scaled
    b0[...] = scaled.astype(BF16)

    bands = [pl.ds(256 * i, 256) for i in range(BLOCK // 256)]

    def newton(m, m_half, m_next, next_half):
        for at in bands:
            b1[at] = (nn(m_half[at], m_half[...]) * 0.0625 - 0.625 * m[at]).astype(BF16)
        for at in bands:
            product = 1.5625 * m[at] + nn(b1[at], m_half[...])
            t0[at] = product
            xr[at] = product.astype(BF16)
        for at in bands:
            product = 1.5625 * t0[at] + nn(b1[at], xr[...])
            m_next[at] = product
            next_half[at] = product.astype(BF16)

    newton(m0, b0, m1, b2)
    newton(m1, b2, m2, b3)

    scale = lax.rsqrt(jnp.sqrt(norm))
    give_half = remote(hbuf, hbuf, ex_send, ex_recv, sibling)
    give_root = remote(xr.at[:, pl.ds(0, HALF)], rbuf, ex_send, ex_recv, sibling)

    @pl.when(core == 0)
    def _():
        starts = [pl.multiple_of((x_ * 2 + zl) * 64, 64) for x_ in (x, x_mirror)]

        def slabs(ref):
            return jnp.concatenate([ref[pl.ds(start, 64), :] for start in starts], axis=0)

        g = nn(slabs(b0), b2[...]) * 0.0625 - 0.3125 * (slabs(m0) + slabs(m1))
        root = 1.25 * g - 0.390625 * slabs(m2) - 0.25 * nn(g.astype(BF16), b3[...])
        row = lax.broadcasted_iota(jnp.int32, (128, BLOCK), 0)
        row = jnp.where(row < 64, row + starts[0], row + (starts[1] - 64))
        column = lax.broadcasted_iota(jnp.int32, (128, BLOCK), 1)
        root = (root + jnp.where(row == column, 1.953125, 0.0)) * scale
        hbuf[...] = nn(root.astype(BF16), u_ref[...]).astype(BF16)
        give_half.start()
        give_half.wait_send()
        give_root.wait_recv()

    @pl.when(core == 1)
    def _():
        for at in bands:
            g = nn(b0[at], b2[...]) * 0.0625 - 0.3125 * (m0[at] + m1[at])
            t0[at] = g
            b1[at] = g.astype(BF16)
        for half in range(2):
            at = pl.ds(half * HALF, HALF)
            root = 1.25 * t0[:, at] - 0.390625 * m2[:, at] - 0.25 * nn(b1[...], b3[:, at])
            t0[:, at] = root
            t0[at, at] = t0[at, at] + jnp.where(eye(HALF), 1.953125, 0.0)
            root = (t0[:, at] * scale).astype(BF16)
            if half:
                rbuf[...] = root
            else:
                xr[:, at] = root
                give_root.start()
        give_root.wait_send()
        give_half.wait_recv()

    def place(row_block, cb):
        lanes = pl.ds(pl.multiple_of(cb * BLOCK + core * HALF, HALF), HALF)
        return upd_ref.at[row_block, :, lanes]

    def landing(dx, dy):
        return place((y + 8 - dy) % 8, 1 - c if dx else c)

    def give(dx, dy):
        remote(osrc.at[dx], place(y, c), o_send, o_recv.at[dx, dy], out_peer(dx, dy)).start()

    def take(dx, dy):
        landed = landing(dx, dy)
        remote(landed, landed, o_send, o_recv.at[dx, dy], sibling).wait_recv()
        remote(landed, landed, of_send, of_recv, sibling).start()

    def hand_on(dx, dy, step):
        landed = landing(dx, dy)
        remote(
            landed, landed, o_send, o_recv.at[dx, (dy + step) % 8], out_peer(0, step % 8)
        ).start()

    piece = (nn(hbuf[...], rbuf[...]) * math.sqrt(BLOCK)).astype(BF16)
    osrc[0] = piece[0:64]
    osrc[1] = piece[64:128]
    for dx, dy in ((1, 2), (1, 6), (0, 2), (0, 6), (1, 1), (1, 7), (0, 1), (0, 7), (1, 0)):
        give(dx, dy)
    remote(osrc.at[0], place(y, c), of_send, of_recv, sibling).start()
    place(y, c)[...] = osrc[0]
    for dx, dy, step in ((0, 2, 1), (0, 6, -1), (1, 2, 1), (1, 6, -1)):
        take(dx, dy)
        if dx == (dy == 6):
            hand_on(dx, dy, 2 * step)
        hand_on(dx, dy, step)
    for dx, dy in ((1, 0), (0, 1), (0, 7), (1, 1), (1, 7), (0, 3), (0, 5), (0, 4), (1, 3), (1, 5), (1, 4)):
        take(dx, dy)
    all_half = upd_ref.at[pl.ds(0, 4)]
    remote(all_half, all_half, of_send, of_recv, sibling).wait()

    remote(y1, y1, y1_send, y1_recv, sibling).wait_send()
    remote(z1, z1, z1_send, z1_recv, sibling).wait_send()
    remote(all_z2, all_z2, z2_send, z2_recv, sibling).wait_send()
    remote(three, three, y2_send, y2_recv, sibling).wait_send()
    remote(three, three, yg_send, yg_recv, sibling).wait_send()
    remote(all_zg, all_zg, zg_send, zg_recv, sibling).wait_send()
    all_out = tile.at[0, pl.ds(0, 3)]
    for _ in range(2):
        remote(all_out, all_out, o_send, y2_recv, sibling).wait_send()
    remote(three, three, o_send, y2_recv, sibling).wait_send()


def on_device(inputs, weight, cotangent):
    square = (BLOCK, BLOCK)
    dma = pltpu.SemaphoreType.DMA
    return pl.pallas_call(
        kernel,
        out_shape=(
            jax.ShapeDtypeStruct((128, 128), BF16),
            jax.ShapeDtypeStruct((8, 64, CB * BLOCK), BF16),
        ),
        in_specs=[pl.BlockSpec(memory_space=pltpu.HBM)] * 3,
        out_specs=(pl.BlockSpec(memory_space=pltpu.VMEM),) * 2,
        scratch_shapes=[
            pltpu.VMEM((128, D), BF16),
            pltpu.VMEM((D, 128), BF16),
            pltpu.VMEM((128, 128), BF16),
            pltpu.VMEM((8, 128, HALF), BF16),
            pltpu.VMEM((128, 128), BF16),
            pltpu.VMEM((8, 4, 16, HALF), BF16),
            pltpu.VMEM((4, 8, 16, HALF), BF16),
            pltpu.VMEM((7, 4, 16, HALF), BF16),
            pltpu.VMEM((3, 8, 16, HALF), BF16),
            pltpu.VMEM((8, 16, HALF), BF16),
            pltpu.VMEM((8, 16, HALF), BF16),
            pltpu.VMEM((4, 4, 16, HALF), BF16),
            pltpu.VMEM((2, 4, 4, 2, 16, HALF), BF16),
            pltpu.VMEM(square, BF16),
            pltpu.VMEM(square, F32),
            pltpu.VMEM(square, F32),
            pltpu.VMEM(square, F32),
            pltpu.VMEM(square, F32),
            pltpu.VMEM(square, BF16),
            pltpu.VMEM(square, BF16),
            pltpu.VMEM(square, BF16),
            pltpu.VMEM(square, BF16),
            pltpu.VMEM(square, BF16),
            pltpu.VMEM((128, BLOCK), BF16),
            pltpu.VMEM((BLOCK, HALF), BF16),
            pltpu.VMEM((2, 64, HALF), BF16),
            dma((3,)),
            dma((8,)), dma((8,)), dma, dma,
            dma, dma, dma, dma, dma, dma, dma, dma,
            dma, dma, dma, dma, dma((2,)), dma((2,)), dma, dma,
            dma, dma((2, 8)), dma, dma,
        ],
        compiler_params=pltpu.CompilerParams(
            collective_id=0, has_side_effects=True, vmem_limit_bytes=48 * 2**20
        ),
    )(*(pltpu.with_memory_space_constraint(v, pltpu.HBM) for v in (inputs, weight, cotangent)))


def solution(mesh):
    placed = (P("dp", None), P(None, "pre"), P("dp", "pre"))
    return jax.shard_map(
        on_device,
        mesh=mesh,
        in_specs=placed,
        out_specs=(P("dp", "pre"), P(None, "pre", None)),
        check_vma=False,
    )
```

```python
import math

import jax
import jax.numpy as jnp
from jax import lax
from jax.experimental import pallas as pl
from jax.experimental.pallas import tpu as pltpu
from jax.sharding import PartitionSpec as P

D = 4096
BLOCK = 512
CB = 2
HALF = BLOCK // 2
DAMPING = 0.1
MESH = pl.DeviceIdType.MESH
BF16 = jnp.bfloat16
F32 = jnp.float32

Y_ORDER = (4, 3, 5, 2, 6, 1, 7, 0)


def nn(a, b):
    return lax.dot_general(a, b, (((1,), (0,)), ((), ())), preferred_element_type=F32)


def nt(a, b):
    return lax.dot_general(a, b, (((1,), (1,)), ((), ())), preferred_element_type=F32)


def kernel(
    a_hbm, w_hbm, b_hbm, out_ref, upd_ref,
    a_v, w_v, b_v, a_s, b_s, part, part_z, y1, z1, zs, z2, y2, tile, u_ref,
    m0, m1, m2, t0, b0, b1, b2, b3, xr, hbuf, rbuf, osrc,
    load_sem, as_send, as_recv, bs_send, bs_recv,
    y1_send, y1_recv, z1_send, z1_recv, z2_send, z2_recv, y2_send, y2_recv,
    yg_send, yg_recv, zg_send, zg_recv, th_send, th_recv, ex_send, ex_recv,
    o_send, o_recv, of_send, of_recv,
):
    dp = lax.axis_index("dp")
    pre = lax.axis_index("pre")
    zh, y, core = dp // 16, (dp // 2) % 8, dp % 2
    x, zl = pre // 2, pre % 2
    z = zh * 2 + zl
    c = x // 2
    x_pair = c * 2 + (1 - x % 2)
    x_mirror = 3 - x

    def dev(zh_, y_, core_, x_, zl_):
        return ((zh_ * 8 + y_) * 2 + core_, x_ * 2 + zl_)

    sibling = dev(zh, y, 1 - core, x, zl)

    def y_peer(dy):
        return dev(zh, (y + dy) % 8, core, x, zl)

    def z_peer(dzh):
        return dev((zh + dzh) % 4, y, core, x, zl)

    def ag_peer(dx, dz):
        z_ = (z + dz) % 8
        return dev(z_ // 2, y, core, x_pair if dx else x, z_ % 2)

    def out_peer(dx, dy):
        return dev(zh, (y + dy) % 8, core, x_mirror if dx else x, zl)

    def remote(src, dst, send, recv, device):
        return pltpu.make_async_remote_copy(
            src_ref=src, dst_ref=dst, send_sem=send, recv_sem=recv,
            device_id=device, device_id_type=MESH,
        )

    load_a = pltpu.make_async_copy(a_hbm, a_v, load_sem.at[0])
    load_b = pltpu.make_async_copy(b_hbm, b_v, load_sem.at[1])
    load_w = pltpu.make_async_copy(w_hbm, w_v, load_sem.at[2])
    load_a.start()
    load_b.start()
    load_w.start()

    barrier = pltpu.get_barrier_semaphore()
    greeted = [ag_peer(dx, dz) for dz in (4, 3, 5, 2, 6, 1, 7, 0) for dx in (1, 0) if dx or dz]
    greeted += [y_peer(dy) for dy in Y_ORDER if dy]
    greeted += [out_peer(1, dy) for dy in (2, 6, 1, 7, 0)]
    greeted += [sibling]
    for device in greeted:
        pl.semaphore_signal(barrier, inc=1, device_id=device, device_id_type=MESH)

    load_a.wait()
    load_b.wait()
    pl.semaphore_wait(barrier, len(greeted))

    def columns(dy, half):
        return pl.ds(pl.multiple_of((y + dy) % 8 * BLOCK + half * HALF, HALF), HALF)

    swap_b = remote(b_v, b_s, bs_send, bs_recv, sibling)
    swap_b.start()
    swaps = {}
    for dy in Y_ORDER:
        swaps[dy] = remote(
            a_v.at[:, columns(dy, 1 - core)], a_s.at[dy], as_send.at[dy], as_recv.at[dy], sibling
        )
        swaps[dy].start()
    swap_b.wait()
    b_t = jnp.concatenate([b_v[...], b_s[...]], axis=0).astype(F32).T.astype(BF16)
    b_t = jnp.concatenate(
        [b_t[h * 32 + path * 16 : h * 32 + path * 16 + 16] for path in range(2) for h in range(4)],
        axis=0,
    )
    def send_y(half, i):
        remote(
            part.at[half, i], y1.at[half, i], y1_send.at[half], y1_recv.at[half], y_peer(Y_ORDER[i])
        ).start()

    def send_z(half, first, count):
        some = pl.ds(first, count)
        for dzh in (1, 3, 2):
            remote(
                part_z.at[half, (zh + dzh) % 4, some], z1.at[half, dzh - 1, some],
                z1_send.at[half], z1_recv.at[half], z_peer(dzh),
            ).start()

    for i, dy in enumerate(Y_ORDER):
        swaps[dy].wait()
        a_both = jnp.concatenate([a_v[:, columns(dy, core)], a_s[dy]], axis=0)
        terms = nn(b_t, a_both).astype(BF16).reshape(2, 4, 16, HALF)
        for half in range(2):
            part[half, i] = terms[0, :, :, half * 128 : half * 128 + 128]
            part_z[half, :, i] = terms[1, :, :, half * 128 : half * 128 + 128]
        if dy:
            send_y(0, i)
        if i % 2:
            send_z(0, i - 1, 2)
    send_z(1, 0, 8)
    for i in range(7):
        send_y(1, i)

    load_w.wait()
    out_ref[...] = nn(a_v[...], w_v[...]).astype(BF16)

    for half in range(2):
        remote(z1.at[half], z1.at[half], z1_send.at[half], z1_recv.at[half], sibling).wait_recv()
        for i, dy in enumerate(Y_ORDER):
            terms = part_z[half, zh, i].astype(F32)
            for dzh in range(3):
                terms += z1[half, dzh, i].astype(F32)
            zs[half, i] = terms.astype(BF16)
            if dy:
                remote(
                    zs.at[half, i], z2.at[half, i], z2_send.at[half], z2_recv.at[half], y_peer(dy)
                ).start()
        remote(y1.at[half], y1.at[half], y1_send.at[half], y1_recv.at[half], sibling).wait_recv()
        total = part[half, 7].astype(F32)
        for i in range(7):
            total += y1[half, i].astype(F32)
        y2[half, zh] = total.astype(BF16)
        for dzh in (2, 1, 3):
            own = y2.at[half, zh]
            remote(own, own, y2_send.at[half], y2_recv.at[half], z_peer(dzh)).start()

    mine = x % 2 * 2 + zl
    for half in range(2):
        all_z2 = z2.at[half, pl.ds(0, 7)]
        remote(all_z2, all_z2, z2_send.at[half], z2_recv.at[half], sibling).wait_recv()
        total = zs[half, 7].astype(F32)
        for i in range(7):
            total += z2[half, i].astype(F32)
        tile[core, half, mine, zh, 1] = total.astype(BF16)
        piece = tile.at[core, half, mine, zh, 1]
        for dx in (1, 0):
            for dz in (4, 3, 5, 2, 6, 1, 7, 0):
                if dx or dz:
                    remote(
                        piece, piece, zg_send.at[half], zg_recv.at[half], ag_peer(dx, dz)
                    ).start()
        three = y2.at[half, pl.ds(0, 3)]
        remote(three, three, y2_send.at[half], y2_recv.at[half], sibling).wait_recv()
        total = y2[half, 0].astype(F32)
        for h in range(1, 4):
            total += y2[half, h].astype(F32)
        tile[core, half, mine, :, 0] = total.astype(BF16)
        piece = tile.at[core, half, mine, :, 0]
        for x_, zl_ in ((x_pair, 1 - zl), (x_pair, zl), (x, 1 - zl)):
            remote(
                piece, piece, yg_send.at[half], yg_recv.at[half], dev(zh, y, core, x_, zl_)
            ).start()

    def swap_tile(half, path):
        ref = tile.at[core, half, :, :, path]
        return remote(ref, ref, th_send.at[half, path], th_recv.at[half, path], sibling)

    for half in range(2):
        three = y2.at[half, pl.ds(0, 3)]
        remote(three, three, yg_send.at[half], yg_recv.at[half], sibling).wait_recv()
        swap_tile(half, 0).start()
        all_zg = z1.at[half, :, pl.ds(0, 5)]
        remote(all_zg, all_zg, zg_send.at[half], zg_recv.at[half], sibling).wait_recv()
        swap_tile(half, 1).start()
    for half in range(2):
        for path in range(2):
            swap_tile(half, path).wait()

    @pl.when(core == 0)
    def _():
        for i in range(4):
            u_ref[i * 128 : i * 128 + 128, :] = tile[i // 2, i % 2].reshape(BLOCK, 128).T

    @pl.when(core == 1)
    def _():
        for i in range(4):
            u_ref[:, i * 128 : i * 128 + 128] = tile[i // 2, i % 2].reshape(BLOCK, 128)

    def eye(n):
        return lax.broadcasted_iota(jnp.int32, (n, n), 0) == lax.broadcasted_iota(
            jnp.int32, (n, n), 1
        )

    t0[...] = nt(u_ref[...], u_ref[...])
    blocks = [pl.ds(128 * i, 128) for i in range(4)]
    trace = sum(jnp.where(eye(128), t0[at, at], 0.0) for at in blocks)
    trace = jnp.sum(trace, keepdims=True)
    shift = DAMPING * trace / BLOCK
    energy = jnp.sum(t0[...] * t0[...], keepdims=True)
    norm = jnp.sqrt(energy + 2.0 * shift * trace + BLOCK * shift * shift)
    for at in blocks:
        t0[at, at] = t0[at, at] + jnp.where(eye(128), shift, 0.0)
    scaled = t0[...] * (1.0 / norm)
    m0[...] = scaled
    b0[...] = scaled.astype(BF16)

    bands = [pl.ds(256 * i, 256) for i in range(BLOCK // 256)]

    def newton(m, m_half, m_next, next_half):
        for at in bands:
            b1[at] = (nn(m_half[at], m_half[...]) * 0.0625 - 0.625 * m[at]).astype(BF16)
        for at in bands:
            product = 1.5625 * m[at] + nn(b1[at], m_half[...])
            t0[at] = product
            xr[at] = product.astype(BF16)
        for at in bands:
            product = 1.5625 * t0[at] + nn(b1[at], xr[...])
            m_next[at] = product
            next_half[at] = product.astype(BF16)

    newton(m0, b0, m1, b2)
    newton(m1, b2, m2, b3)

    scale = lax.rsqrt(jnp.sqrt(norm))
    give_half = remote(hbuf, hbuf, ex_send, ex_recv, sibling)
    give_root = remote(xr.at[:, pl.ds(0, HALF)], rbuf, ex_send, ex_recv, sibling)

    @pl.when(core == 0)
    def _():
        starts = [pl.multiple_of((x_ * 2 + zl) * 64, 64) for x_ in (x, x_mirror)]

        def slabs(ref):
            return jnp.concatenate([ref[pl.ds(start, 64), :] for start in starts], axis=0)

        g = nn(slabs(b0), b2[...]) * 0.0625 - 0.3125 * (slabs(m0) + slabs(m1))
        root = 1.25 * g - 0.390625 * slabs(m2) - 0.25 * nn(g.astype(BF16), b3[...])
        row = lax.broadcasted_iota(jnp.int32, (128, BLOCK), 0)
        row = jnp.where(row < 64, row + starts[0], row + (starts[1] - 64))
        column = lax.broadcasted_iota(jnp.int32, (128, BLOCK), 1)
        root = (root + jnp.where(row == column, 1.953125, 0.0)) * scale
        hbuf[...] = nn(root.astype(BF16), u_ref[...]).astype(BF16)
        give_half.start()
        give_half.wait_send()
        give_root.wait_recv()

    @pl.when(core == 1)
    def _():
        for at in bands:
            g = nn(b0[at], b2[...]) * 0.0625 - 0.3125 * (m0[at] + m1[at])
            t0[at] = g
            b1[at] = g.astype(BF16)
        for half in range(2):
            at = pl.ds(half * HALF, HALF)
            root = 1.25 * t0[:, at] - 0.390625 * m2[:, at] - 0.25 * nn(b1[...], b3[:, at])
            t0[:, at] = root
            t0[at, at] = t0[at, at] + jnp.where(eye(HALF), 1.953125, 0.0)
            root = (t0[:, at] * scale).astype(BF16)
            if half:
                rbuf[...] = root
            else:
                xr[:, at] = root
                give_root.start()
        give_root.wait_send()
        give_half.wait_recv()

    def place(row_block, cb):
        lanes = pl.ds(pl.multiple_of(cb * BLOCK + core * HALF, HALF), HALF)
        return upd_ref.at[row_block, :, lanes]

    def landing(dx, dy):
        return place((y + 8 - dy) % 8, 1 - c if dx else c)

    def give(dx, dy):
        remote(osrc.at[dx], place(y, c), o_send, o_recv.at[dx, dy], out_peer(dx, dy)).start()

    def take(dx, dy):
        landed = landing(dx, dy)
        remote(landed, landed, o_send, o_recv.at[dx, dy], sibling).wait_recv()

    def share(dx, dy):
        landed = landing(dx, dy)
        remote(landed, landed, of_send, of_recv, sibling).start()

    def hand_on(dx, dy, step):
        landed = landing(dx, dy)
        remote(
            landed, landed, o_send, o_recv.at[dx, (dy + step) % 8], out_peer(0, step % 8)
        ).start()

    piece = (nn(hbuf[...], rbuf[...]) * math.sqrt(BLOCK)).astype(BF16)
    osrc[0] = piece[0:64]
    osrc[1] = piece[64:128]
    for dx, dy in ((1, 2), (1, 6), (0, 2), (0, 6), (1, 1), (1, 7), (0, 1), (0, 7), (1, 0)):
        give(dx, dy)
    remote(osrc.at[0], place(y, c), of_send, of_recv, sibling).start()
    place(y, c)[...] = osrc[0]
    for dx, dy, step in ((0, 2, 1), (0, 6, -1), (1, 2, 1), (1, 6, -1)):
        take(dx, dy)
        if dx == (dy == 6):
            hand_on(dx, dy, 2 * step)
        hand_on(dx, dy, step)
        share(dx, dy)
    for dx, dy in ((1, 0), (0, 1), (0, 7), (1, 1), (1, 7), (0, 3), (0, 5), (1, 3), (1, 5), (0, 4), (1, 4)):
        take(dx, dy)
        share(dx, dy)
    all_half = upd_ref.at[pl.ds(0, 4)]
    remote(all_half, all_half, of_send, of_recv, sibling).wait()

    for half in range(2):
        all_z2 = z2.at[half, pl.ds(0, 7)]
        three = y2.at[half, pl.ds(0, 3)]
        all_zg = z1.at[half, :, pl.ds(0, 5)]
        for sent, sem in (
            (y1.at[half], y1_send), (z1.at[half], z1_send), (all_z2, z2_send),
            (three, y2_send), (three, yg_send), (all_zg, zg_send),
        ):
            remote(sent, sent, sem.at[half], th_recv.at[0, 0], sibling).wait_send()
    for sent in (tile.at[0, 0], tile.at[0, 0], tile.at[0, 1], tile.at[0, 0, pl.ds(0, 3)]):
        remote(sent, sent, o_send, th_recv.at[0, 0], sibling).wait_send()


def on_device(inputs, weight, cotangent):
    square = (BLOCK, BLOCK)
    dma = pltpu.SemaphoreType.DMA
    return pl.pallas_call(
        kernel,
        out_shape=(
            jax.ShapeDtypeStruct((128, 128), BF16),
            jax.ShapeDtypeStruct((8, 64, CB * BLOCK), BF16),
        ),
        in_specs=[pl.BlockSpec(memory_space=pltpu.HBM)] * 3,
        out_specs=(pl.BlockSpec(memory_space=pltpu.VMEM),) * 2,
        scratch_shapes=[
            pltpu.VMEM((128, D), BF16),
            pltpu.VMEM((D, 128), BF16),
            pltpu.VMEM((128, 128), BF16),
            pltpu.VMEM((8, 128, HALF), BF16),
            pltpu.VMEM((128, 128), BF16),
            pltpu.VMEM((2, 8, 4, 16, 128), BF16),
            pltpu.VMEM((2, 4, 8, 16, 128), BF16),
            pltpu.VMEM((2, 7, 4, 16, 128), BF16),
            pltpu.VMEM((2, 3, 8, 16, 128), BF16),
            pltpu.VMEM((2, 8, 16, 128), BF16),
            pltpu.VMEM((2, 8, 16, 128), BF16),
            pltpu.VMEM((2, 4, 4, 16, 128), BF16),
            pltpu.VMEM((2, 2, 4, 4, 2, 16, 128), BF16),
            pltpu.VMEM(square, BF16),
            pltpu.VMEM(square, F32),
            pltpu.VMEM(square, F32),
            pltpu.VMEM(square, F32),
            pltpu.VMEM(square, F32),
            pltpu.VMEM(square, BF16),
            pltpu.VMEM(square, BF16),
            pltpu.VMEM(square, BF16),
            pltpu.VMEM(square, BF16),
            pltpu.VMEM(square, BF16),
            pltpu.VMEM((128, BLOCK), BF16),
            pltpu.VMEM((BLOCK, HALF), BF16),
            pltpu.VMEM((2, 64, HALF), BF16),
            dma((3,)),
            dma((8,)), dma((8,)), dma, dma,
            *[dma((2,))] * 12,
            dma((2, 2)), dma((2, 2)), dma, dma,
            dma, dma((2, 8)), dma, dma,
        ],
        compiler_params=pltpu.CompilerParams(
            collective_id=0, has_side_effects=True, vmem_limit_bytes=48 * 2**20
        ),
    )(*(pltpu.with_memory_space_constraint(v, pltpu.HBM) for v in (inputs, weight, cotangent)))


def solution(mesh):
    placed = (P("dp", None), P(None, "pre"), P("dp", "pre"))
    return jax.shard_map(
        on_device,
        mesh=mesh,
        in_specs=placed,
        out_specs=(P("dp", "pre"), P(None, "pre", None)),
        check_vma=False,
    )
```

```python
import math

import jax
import jax.numpy as jnp
from jax import lax
from jax.experimental import pallas as pl
from jax.experimental.pallas import tpu as pltpu
from jax.sharding import PartitionSpec as P

D = 4096
BLOCK = 512
CB = 2
HALF = BLOCK // 2
DAMPING = 0.1
MESH = pl.DeviceIdType.MESH
BF16 = jnp.bfloat16
F32 = jnp.float32

Y_ORDER = (4, 3, 5, 2, 6, 1, 7, 0)


def nn(a, b):
    return lax.dot_general(a, b, (((1,), (0,)), ((), ())), preferred_element_type=F32)


def nt(a, b):
    return lax.dot_general(a, b, (((1,), (1,)), ((), ())), preferred_element_type=F32)


def kernel(
    a_hbm, w_hbm, b_hbm, out_ref, upd_ref,
    a_v, w_v, b_v, give, got, kept, part, part_z, y1, z1, zs, z2, y2, tile, u_ref,
    m0, m1, m2, t0, b0, b1, b2, b3, xr, hbuf, osrc,
    load_sem, sw_send, sw_recv,
    y1_send, y1_recv, z1_send, z1_recv, z2_send, z2_recv, y2_send, y2_recv,
    yg_send, yg_recv, zg_send, zg_recv, th_send, th_recv, ex_send, ex_recv,
    o_send, o_recv, of_send, of_recv,
):
    dp = lax.axis_index("dp")
    pre = lax.axis_index("pre")
    zh, y, core = lax.div(dp, 16), lax.rem(lax.div(dp, 2), 8), lax.rem(dp, 2)
    x, zl = lax.div(pre, 2), lax.rem(pre, 2)
    z = zh * 2 + zl
    c = lax.div(x, 2)
    x_pair = c * 2 + (1 - lax.rem(x, 2))
    x_mirror = 3 - x

    def dev(zh_, y_, core_, x_, zl_):
        return ((zh_ * 8 + y_) * 2 + core_, x_ * 2 + zl_)

    sibling = dev(zh, y, 1 - core, x, zl)

    def y_peer(dy):
        return dev(zh, lax.rem(y + dy, 8), core, x, zl)

    def z_peer(dzh):
        return dev(lax.rem(zh + dzh, 4), y, core, x, zl)

    def ag_peer(dx, dz):
        z_ = lax.rem(z + dz, 8)
        return dev(lax.div(z_, 2), y, core, x_pair if dx else x, lax.rem(z_, 2))

    def out_peer(dx, dy):
        return dev(zh, lax.rem(y + dy, 8), core, x_mirror if dx else x, zl)

    def remote(src, dst, send, recv, device):
        return pltpu.make_async_remote_copy(
            src_ref=src, dst_ref=dst, send_sem=send, recv_sem=recv,
            device_id=device, device_id_type=MESH,
        )

    def load_a(i):
        at = pl.ds(pl.multiple_of(lax.rem(y + Y_ORDER[i], 8) * BLOCK, BLOCK), BLOCK)
        return pltpu.make_async_copy(a_hbm.at[:, at], a_v.at[:, at], load_sem.at[i])

    load_b = pltpu.make_async_copy(b_hbm, b_v, load_sem.at[8])
    load_w = pltpu.make_async_copy(w_hbm, w_v, load_sem.at[9])
    load_b.start()
    for i in range(8):
        load_a(i).start()

    barrier = pltpu.get_barrier_semaphore()
    greeted = [ag_peer(dx, dz) for dz in (4, 3, 5, 2, 6, 1, 7, 0) for dx in (1, 0) if dx or dz]
    greeted += [y_peer(dy) for dy in Y_ORDER if dy]
    greeted += [out_peer(1, dy) for dy in (2, 6, 1, 7, 0)]
    greeted += [sibling]
    for device in greeted:
        pl.semaphore_signal(barrier, inc=1, device_id=device, device_id_type=MESH)

    def columns(dy, half):
        return pl.ds(pl.multiple_of(lax.rem(y + dy, 8) * BLOCK + half * HALF, HALF), HALF)

    load_b.wait()
    b_t = b_v[...].astype(F32).T.astype(BF16)
    b_t = jnp.concatenate(
        [b_t[h * 32 + path * 16 : h * 32 + path * 16 + 16] for path in range(2) for h in range(4)],
        axis=0,
    )
    for i, dy in enumerate(Y_ORDER):
        load_a(i).wait()
        terms = nn(b_t, a_v[:, columns(dy, 1 - core)]).astype(BF16)
        give[0, i] = terms[:, 0:128]
        give[1, i] = terms[:, 128:HALF]
        kept[i] = nn(b_t, a_v[:, columns(dy, core)])
    load_w.start()
    pl.semaphore_wait(barrier, len(greeted))

    def swap(half, pair):
        some = pl.ds(2 * pair, 2)
        return remote(
            give.at[half, some], got.at[half, some], sw_send.at[half, pair], sw_recv.at[half, pair],
            sibling,
        )

    for pair in range(4):
        swap(0, pair).start()

    def send_y(half, i):
        remote(
            part.at[half, i], y1.at[half, i], y1_send.at[half], y1_recv.at[half], y_peer(Y_ORDER[i])
        ).start()

    def send_z(half, first, count):
        some = pl.ds(first, count)
        for dzh in (1, 3, 2):
            remote(
                part_z.at[half, lax.rem(zh + dzh, 4), some], z1.at[half, dzh - 1, some],
                z1_send.at[half], z1_recv.at[half], z_peer(dzh),
            ).start()

    for half in range(2):
        for pair in range(4):
            swap(half, pair).wait()
            for i in (2 * pair, 2 * pair + 1):
                lanes = pl.ds(half * 128, 128)
                terms = (kept[i, :, lanes] + got[half, i].astype(F32)).astype(BF16)
                terms = terms.reshape(2, 4, 16, 128)
                part[half, i] = terms[0]
                part_z[half, :, i] = terms[1]
            if half == 0:
                send_z(half, 2 * pair, 2)
                swap(1, pair).start()
                for i in (2 * pair, 2 * pair + 1):
                    if Y_ORDER[i]:
                        send_y(half, i)
            else:
                if pair % 2:
                    send_z(half, 2 * pair - 2, 4)
                for i in (2 * pair, 2 * pair + 1):
                    if Y_ORDER[i]:
                        send_y(half, i)

    load_w.wait()
    out_ref[...] = nn(a_v[...], w_v[...]).astype(BF16)

    for half in range(2):
        remote(z1.at[half], z1.at[half], z1_send.at[half], z1_recv.at[half], sibling).wait_recv()
        for i, dy in enumerate(Y_ORDER):
            terms = part_z[half, zh, i].astype(F32)
            for dzh in range(3):
                terms += z1[half, dzh, i].astype(F32)
            zs[half, i] = terms.astype(BF16)
            if dy:
                remote(
                    zs.at[half, i], z2.at[half, i], z2_send.at[half], z2_recv.at[half], y_peer(dy)
                ).start()
        remote(y1.at[half], y1.at[half], y1_send.at[half], y1_recv.at[half], sibling).wait_recv()
        total = part[half, 7].astype(F32)
        for i in range(7):
            total += y1[half, i].astype(F32)
        y2[half, zh] = total.astype(BF16)
        for dzh in (2, 1, 3):
            own = y2.at[half, zh]
            remote(own, own, y2_send.at[half], y2_recv.at[half], z_peer(dzh)).start()

    mine = lax.rem(x, 2) * 2 + zl
    for half in range(2):
        all_z2 = z2.at[half, pl.ds(0, 7)]
        remote(all_z2, all_z2, z2_send.at[half], z2_recv.at[half], sibling).wait_recv()
        total = zs[half, 7].astype(F32)
        for i in range(7):
            total += z2[half, i].astype(F32)
        tile[core, half, mine, zh, 1] = total.astype(BF16)
        piece = tile.at[core, half, mine, zh, 1]
        for dx in (1, 0):
            for dz in (4, 3, 5, 2, 6, 1, 7, 0):
                if dx or dz:
                    remote(
                        piece, piece, zg_send.at[half], zg_recv.at[half], ag_peer(dx, dz)
                    ).start()
        three = y2.at[half, pl.ds(0, 3)]
        remote(three, three, y2_send.at[half], y2_recv.at[half], sibling).wait_recv()
        total = y2[half, 0].astype(F32)
        for h in range(1, 4):
            total += y2[half, h].astype(F32)
        tile[core, half, mine, :, 0] = total.astype(BF16)
        piece = tile.at[core, half, mine, :, 0]
        for x_, zl_ in ((x_pair, 1 - zl), (x_pair, zl), (x, 1 - zl)):
            remote(
                piece, piece, yg_send.at[half], yg_recv.at[half], dev(zh, y, core, x_, zl_)
            ).start()

    def swap_tile(half, path):
        ref = tile.at[core, half, :, :, path]
        return remote(ref, ref, th_send.at[half, path], th_recv.at[half, path], sibling)

    for half in range(2):
        three = y2.at[half, pl.ds(0, 3)]
        remote(three, three, yg_send.at[half], yg_recv.at[half], sibling).wait_recv()
        swap_tile(half, 0).start()
        all_zg = z1.at[half, :, pl.ds(0, 5)]
        remote(all_zg, all_zg, zg_send.at[half], zg_recv.at[half], sibling).wait_recv()
        swap_tile(half, 1).start()
    for half in range(2):
        for path in range(2):
            swap_tile(half, path).wait()

    @pl.when(core == 0)
    def _():
        for i in range(4):
            u_ref[i * 128 : i * 128 + 128, :] = tile[i // 2, i % 2].reshape(BLOCK, 128).T

    @pl.when(core == 1)
    def _():
        for i in range(4):
            u_ref[:, i * 128 : i * 128 + 128] = tile[i // 2, i % 2].reshape(BLOCK, 128)

    def eye(n):
        return lax.broadcasted_iota(jnp.int32, (n, n), 0) == lax.broadcasted_iota(
            jnp.int32, (n, n), 1
        )

    t0[...] = nt(u_ref[...], u_ref[...])
    blocks = [pl.ds(128 * i, 128) for i in range(4)]
    trace = sum(jnp.where(eye(128), t0[at, at], 0.0) for at in blocks)
    trace = jnp.sum(trace, keepdims=True)
    shift = DAMPING * trace / BLOCK
    energy = jnp.sum(t0[...] * t0[...], keepdims=True)
    norm = jnp.sqrt(energy + 2.0 * shift * trace + BLOCK * shift * shift)
    for at in blocks:
        t0[at, at] = t0[at, at] + jnp.where(eye(128), shift, 0.0)
    scaled = t0[...] * (1.0 / norm)
    m0[...] = scaled
    b0[...] = scaled.astype(BF16)

    bands = [pl.ds(256 * i, 256) for i in range(BLOCK // 256)]

    def newton(m, m_half, m_next, next_half):
        for at in bands:
            b1[at] = (nn(m_half[at], m_half[...]) * 0.0625 - 0.625 * m[at]).astype(BF16)
        for at in bands:
            product = 1.5625 * m[at] + nn(b1[at], m_half[...])
            t0[at] = product
            xr[at] = product.astype(BF16)
        for at in bands:
            product = 1.5625 * t0[at] + nn(b1[at], xr[...])
            m_next[at] = product
            next_half[at] = product.astype(BF16)

    newton(m0, b0, m1, b2)
    newton(m1, b2, m2, b3)

    scale = lax.rsqrt(jnp.sqrt(norm))
    give_half = remote(hbuf, hbuf, ex_send, ex_recv, sibling)

    @pl.when(core == 0)
    def _():
        starts = [pl.multiple_of((x_ * 2 + zl) * 64, 64) for x_ in (x, x_mirror)]

        def slabs(ref):
            return jnp.concatenate([ref[pl.ds(start, 64), :] for start in starts], axis=0)

        g = nn(slabs(b0), b2[...]) * 0.0625 - 0.3125 * (slabs(m0) + slabs(m1))
        root = 1.25 * g - 0.390625 * slabs(m2) - 0.25 * nn(g.astype(BF16), b3[...])
        row = lax.broadcasted_iota(jnp.int32, (128, BLOCK), 0)
        row = jnp.where(row < 64, row + starts[0], row + (starts[1] - 64))
        column = lax.broadcasted_iota(jnp.int32, (128, BLOCK), 1)
        root = (root + jnp.where(row == column, 1.953125, 0.0)) * scale
        hbuf[...] = nn(root.astype(BF16), u_ref[...]).astype(BF16)
        give_half.start()
        give_half.wait_send()

    @pl.when(core == 1)
    def _():
        for at in bands:
            g = nn(b0[at], b2[...]) * 0.0625 - 0.3125 * (m0[at] + m1[at])
            t0[at] = g
            b1[at] = g.astype(BF16)
        for half in range(2):
            at = pl.ds(half * HALF, HALF)
            root = 1.25 * t0[:, at] - 0.390625 * m2[:, at] - 0.25 * nn(b1[...], b3[:, at])
            t0[:, at] = root
            t0[at, at] = t0[at, at] + jnp.where(eye(HALF), 1.953125, 0.0)
            xr[:, at] = (t0[:, at] * scale).astype(BF16)
        give_half.wait_recv()
        piece = (nn(hbuf[...], xr[...]) * math.sqrt(BLOCK)).astype(BF16)
        osrc[0] = piece[0:64]
        osrc[1] = piece[64:128]

    def place(row_block, cb):
        lanes = pl.ds(pl.multiple_of(cb * BLOCK, BLOCK), BLOCK)
        return upd_ref.at[row_block, :, lanes]

    def landing(dx, dy):
        return place(lax.rem(y + 8 - dy, 8), 1 - c if dx else c)

    def send_out(dx, dy):
        remote(osrc.at[dx], place(y, c), o_send, o_recv.at[dx, dy], out_peer(dx, dy)).start()

    def take(dx, dy):
        landed = landing(dx, dy)
        remote(landed, landed, o_send, o_recv.at[dx, dy], sibling).wait_recv()

    def share(dx, dy):
        landed = landing(dx, dy)
        remote(landed, landed, of_send, of_recv, sibling).start()

    def hand_on(dx, dy, step):
        landed = landing(dx, dy)
        remote(
            landed, landed, o_send, o_recv.at[dx, (dy + step) % 8], out_peer(0, step % 8)
        ).start()

    @pl.when(core == 1)
    def _():
        for dx, dy in ((1, 2), (1, 6), (0, 2), (0, 6), (1, 1), (1, 7), (0, 1), (0, 7), (1, 0)):
            send_out(dx, dy)
        remote(osrc.at[0], place(y, c), of_send, of_recv, sibling).start()
        place(y, c)[...] = osrc[0]
        for dx, dy, step in ((0, 2, 1), (0, 6, -1), (1, 2, 1), (1, 6, -1)):
            take(dx, dy)
            if dx == (dy == 6):
                hand_on(dx, dy, 2 * step)
            hand_on(dx, dy, step)
            share(dx, dy)
        for dx, dy in ((1, 0), (0, 1), (0, 7), (1, 1), (1, 7), (0, 3), (0, 5), (1, 3), (1, 5), (0, 4), (1, 4)):
            take(dx, dy)
            share(dx, dy)
        for sent in [tile.at[0]] * 3 + [tile.at[0, 0], tile.at[0, 0, pl.ds(0, 2)]]:
            remote(sent, sent, o_send, th_recv.at[0, 0], sibling).wait_send()
        remote(upd_ref, upd_ref, of_send, of_recv, sibling).wait_send()

    @pl.when(core == 0)
    def _():
        remote(upd_ref, upd_ref, of_send, of_recv, sibling).wait_recv()

    for half in range(2):
        all_z2 = z2.at[half, pl.ds(0, 7)]
        three = y2.at[half, pl.ds(0, 3)]
        all_zg = z1.at[half, :, pl.ds(0, 5)]
        for sent, sem in (
            (y1.at[half], y1_send), (z1.at[half], z1_send), (all_z2, z2_send),
            (three, y2_send), (three, yg_send), (all_zg, zg_send),
        ):
            remote(sent, sent, sem.at[half], th_recv.at[0, 0], sibling).wait_send()


def on_device(inputs, weight, cotangent):
    square = (BLOCK, BLOCK)
    dma = pltpu.SemaphoreType.DMA
    return pl.pallas_call(
        kernel,
        out_shape=(
            jax.ShapeDtypeStruct((128, 128), BF16),
            jax.ShapeDtypeStruct((8, 64, CB * BLOCK), BF16),
        ),
        in_specs=[pl.BlockSpec(memory_space=pltpu.HBM)] * 3,
        out_specs=(pl.BlockSpec(memory_space=pltpu.VMEM),) * 2,
        scratch_shapes=[
            pltpu.VMEM((128, D), BF16),
            pltpu.VMEM((D, 128), BF16),
            pltpu.VMEM((128, 128), BF16),
            pltpu.VMEM((2, 8, 128, 128), BF16),
            pltpu.VMEM((2, 8, 128, 128), BF16),
            pltpu.VMEM((8, 128, HALF), F32),
            pltpu.VMEM((2, 8, 4, 16, 128), BF16),
            pltpu.VMEM((2, 4, 8, 16, 128), BF16),
            pltpu.VMEM((2, 7, 4, 16, 128), BF16),
            pltpu.VMEM((2, 3, 8, 16, 128), BF16),
            pltpu.VMEM((2, 8, 16, 128), BF16),
            pltpu.VMEM((2, 8, 16, 128), BF16),
            pltpu.VMEM((2, 4, 4, 16, 128), BF16),
            pltpu.VMEM((2, 2, 4, 4, 2, 16, 128), BF16),
            pltpu.VMEM(square, BF16),
            pltpu.VMEM(square, F32),
            pltpu.VMEM(square, F32),
            pltpu.VMEM(square, F32),
            pltpu.VMEM(square, F32),
            pltpu.VMEM(square, BF16),
            pltpu.VMEM(square, BF16),
            pltpu.VMEM(square, BF16),
            pltpu.VMEM(square, BF16),
            pltpu.VMEM(square, BF16),
            pltpu.VMEM((128, BLOCK), BF16),
            pltpu.VMEM((2, 64, BLOCK), BF16),
            dma((10,)),
            dma((2, 4)), dma((2, 4)),
            *[dma((2,))] * 12,
            dma((2, 2)), dma((2, 2)), dma, dma,
            dma, dma((2, 8)), dma, dma,
        ],
        compiler_params=pltpu.CompilerParams(
            collective_id=0, has_side_effects=True, vmem_limit_bytes=48 * 2**20
        ),
    )(*(pltpu.with_memory_space_constraint(v, pltpu.HBM) for v in (inputs, weight, cotangent)))


def solution(mesh):
    placed = (P("dp", None), P(None, "pre"), P("dp", "pre"))
    return jax.shard_map(
        on_device,
        mesh=mesh,
        in_specs=placed,
        out_specs=(P("dp", "pre"), P(None, "pre", None)),
        check_vma=False,
    )
```

```python
import math

import jax
import jax.numpy as jnp
from jax import lax
from jax.experimental import pallas as pl
from jax.experimental.pallas import tpu as pltpu
from jax.sharding import PartitionSpec as P

D = 4096
BLOCK = 512
CB = 2
HALF = BLOCK // 2
DAMPING = 0.1
MESH = pl.DeviceIdType.MESH
BF16 = jnp.bfloat16
F32 = jnp.float32

Y_ORDER = (4, 3, 5, 2, 6, 1, 7, 0)


def nn(a, b):
    return lax.dot_general(a, b, (((1,), (0,)), ((), ())), preferred_element_type=F32)


def nt(a, b):
    return lax.dot_general(a, b, (((1,), (1,)), ((), ())), preferred_element_type=F32)


def kernel(
    a_hbm, w_hbm, b_hbm, out_ref, upd_ref,
    a_v, w_v, b_v, give, got, kept, part, part_z, y1, z1, zs, z2, y2, tile, u_ref,
    m0, m1, m2, t0, b0, b1, b2, b3, xr, hbuf, osrc,
    load_sem, sw_send, sw_recv,
    y1_send, y1_recv, z1_send, z1_recv, z2_send, z2_recv, y2_send, y2_recv,
    yg_send, yg_recv, zg_send, zg_recv, th_send, th_recv, ex_send, ex_recv,
    o_send, o_recv, of_send, of_recv,
):
    dp = lax.axis_index("dp")
    pre = lax.axis_index("pre")
    zh, y, core = lax.div(dp, 16), lax.rem(lax.div(dp, 2), 8), lax.rem(dp, 2)
    x, zl = lax.div(pre, 2), lax.rem(pre, 2)
    z = zh * 2 + zl
    c = lax.div(x, 2)
    x_pair = c * 2 + (1 - lax.rem(x, 2))
    x_mirror = 3 - x

    def dev(zh_, y_, core_, x_, zl_):
        return ((zh_ * 8 + y_) * 2 + core_, x_ * 2 + zl_)

    sibling = dev(zh, y, 1 - core, x, zl)

    def y_peer(dy):
        return dev(zh, lax.rem(y + dy, 8), core, x, zl)

    def z_peer(dzh):
        return dev(lax.rem(zh + dzh, 4), y, core, x, zl)

    def ag_peer(dx, dz):
        z_ = lax.rem(z + dz, 8)
        return dev(lax.div(z_, 2), y, core, x_pair if dx else x, lax.rem(z_, 2))

    def out_peer(dx, dy):
        return dev(zh, lax.rem(y + dy, 8), core, x_mirror if dx else x, zl)

    def remote(src, dst, send, recv, device):
        return pltpu.make_async_remote_copy(
            src_ref=src, dst_ref=dst, send_sem=send, recv_sem=recv,
            device_id=device, device_id_type=MESH,
        )

    def load_a(i):
        at = pl.ds(pl.multiple_of(lax.rem(y + Y_ORDER[i], 8) * BLOCK, BLOCK), BLOCK)
        return pltpu.make_async_copy(a_hbm.at[:, at], a_v.at[:, at], load_sem.at[i])

    load_b = pltpu.make_async_copy(b_hbm, b_v, load_sem.at[8])
    load_w = pltpu.make_async_copy(w_hbm, w_v, load_sem.at[9])
    load_b.start()
    for i in range(8):
        load_a(i).start()

    barrier = pltpu.get_barrier_semaphore()
    greeted = [ag_peer(dx, dz) for dz in (4, 3, 5, 2, 6, 1, 7, 0) for dx in (1, 0) if dx or dz]
    greeted += [y_peer(dy) for dy in Y_ORDER if dy]
    greeted += [out_peer(1, dy) for dy in (2, 6, 1, 7, 0)]
    greeted += [sibling]
    for device in greeted:
        pl.semaphore_signal(barrier, inc=1, device_id=device, device_id_type=MESH)

    def columns(dy, half):
        return pl.ds(pl.multiple_of(lax.rem(y + dy, 8) * BLOCK + half * HALF, HALF), HALF)

    load_b.wait()
    b_t = b_v[...].astype(F32).T.astype(BF16)
    b_t = jnp.concatenate(
        [b_t[h * 32 + path * 16 : h * 32 + path * 16 + 16] for path in range(2) for h in range(4)],
        axis=0,
    )
    for i, dy in enumerate(Y_ORDER):
        load_a(i).wait()
        terms = nn(b_t, a_v[:, columns(dy, 1 - core)]).astype(BF16)
        give[0, i] = terms[:, 0:128]
        give[1, i] = terms[:, 128:HALF]
        kept[i] = nn(b_t, a_v[:, columns(dy, core)])
    load_w.start()
    pl.semaphore_wait(barrier, len(greeted))

    def swap(half, pair):
        some = pl.ds(2 * pair, 2)
        return remote(
            give.at[half, some], got.at[half, some], sw_send.at[half, pair], sw_recv.at[half, pair],
            sibling,
        )

    for pair in range(4):
        swap(0, pair).start()

    def send_y(half, i):
        remote(
            part.at[half, i], y1.at[half, i], y1_send.at[half], y1_recv.at[half], y_peer(Y_ORDER[i])
        ).start()

    def send_z(half, first, count):
        some = pl.ds(first, count)
        for dzh in (2, 1, 3):
            remote(
                part_z.at[half, lax.rem(zh + dzh, 4), some], z1.at[half, dzh - 1, some],
                z1_send.at[half], z1_recv.at[half], z_peer(dzh),
            ).start()

    for half in range(2):
        for pair in range(4):
            swap(half, pair).wait()
            for i in (2 * pair, 2 * pair + 1):
                lanes = pl.ds(half * 128, 128)
                terms = (kept[i, :, lanes] + got[half, i].astype(F32)).astype(BF16)
                terms = terms.reshape(2, 4, 16, 128)
                part[half, i] = terms[0]
                part_z[half, :, i] = terms[1]
            if half == 0:
                send_z(half, 2 * pair, 2)
                swap(1, pair).start()
                for i in (2 * pair, 2 * pair + 1):
                    if Y_ORDER[i]:
                        send_y(half, i)
            else:
                if pair % 2:
                    send_z(half, 2 * pair - 2, 4)
                for i in (2 * pair, 2 * pair + 1):
                    if Y_ORDER[i]:
                        send_y(half, i)

    load_w.wait()
    out_ref[...] = nn(a_v[...], w_v[...]).astype(BF16)

    for half in range(2):
        remote(z1.at[half], z1.at[half], z1_send.at[half], z1_recv.at[half], sibling).wait_recv()
        for i, dy in enumerate(Y_ORDER):
            terms = part_z[half, zh, i].astype(F32)
            for dzh in range(3):
                terms += z1[half, dzh, i].astype(F32)
            zs[half, i] = terms.astype(BF16)
            if dy:
                remote(
                    zs.at[half, i], z2.at[half, i], z2_send.at[half], z2_recv.at[half], y_peer(dy)
                ).start()
        remote(y1.at[half], y1.at[half], y1_send.at[half], y1_recv.at[half], sibling).wait_recv()
        total = part[half, 7].astype(F32)
        for i in range(7):
            total += y1[half, i].astype(F32)
        y2[half, zh] = total.astype(BF16)
        for dzh in (2, 1, 3):
            own = y2.at[half, zh]
            remote(own, own, y2_send.at[half], y2_recv.at[half], z_peer(dzh)).start()

    mine = lax.rem(x, 2) * 2 + zl
    for half in range(2):
        all_z2 = z2.at[half, pl.ds(0, 7)]
        remote(all_z2, all_z2, z2_send.at[half], z2_recv.at[half], sibling).wait_recv()
        total = zs[half, 7].astype(F32)
        for i in range(7):
            total += z2[half, i].astype(F32)
        tile[core, half, mine, zh, 1] = total.astype(BF16)
        piece = tile.at[core, half, mine, zh, 1]
        for dz in (4, 3, 5, 2, 6, 1, 7, 0):
            for dx in (1, 0):
                if dx or dz:
                    remote(
                        piece, piece, zg_send.at[half], zg_recv.at[half], ag_peer(dx, dz)
                    ).start()
        three = y2.at[half, pl.ds(0, 3)]
        remote(three, three, y2_send.at[half], y2_recv.at[half], sibling).wait_recv()
        total = y2[half, 0].astype(F32)
        for h in range(1, 4):
            total += y2[half, h].astype(F32)
        tile[core, half, mine, :, 0] = total.astype(BF16)
        piece = tile.at[core, half, mine, :, 0]
        for x_, zl_ in ((x_pair, 1 - zl), (x_pair, zl), (x, 1 - zl)):
            remote(
                piece, piece, yg_send.at[half], yg_recv.at[half], dev(zh, y, core, x_, zl_)
            ).start()

    def swap_tile(half, path):
        ref = tile.at[core, half, :, :, path]
        return remote(ref, ref, th_send.at[half, path], th_recv.at[half, path], sibling)

    for half in range(2):
        three = y2.at[half, pl.ds(0, 3)]
        remote(three, three, yg_send.at[half], yg_recv.at[half], sibling).wait_recv()
        swap_tile(half, 0).start()
        all_zg = z1.at[half, :, pl.ds(0, 5)]
        remote(all_zg, all_zg, zg_send.at[half], zg_recv.at[half], sibling).wait_recv()
        swap_tile(half, 1).start()
    for half in range(2):
        for path in range(2):
            swap_tile(half, path).wait()

    @pl.when(core == 0)
    def _():
        for i in range(4):
            u_ref[i * 128 : i * 128 + 128, :] = tile[i // 2, i % 2].reshape(BLOCK, 128).T

    @pl.when(core == 1)
    def _():
        for i in range(4):
            u_ref[:, i * 128 : i * 128 + 128] = tile[i // 2, i % 2].reshape(BLOCK, 128)

    def eye(n):
        return lax.broadcasted_iota(jnp.int32, (n, n), 0) == lax.broadcasted_iota(
            jnp.int32, (n, n), 1
        )

    t0[...] = nt(u_ref[...], u_ref[...])
    blocks = [pl.ds(128 * i, 128) for i in range(4)]
    trace = sum(jnp.where(eye(128), t0[at, at], 0.0) for at in blocks)
    trace = jnp.sum(trace, keepdims=True)
    shift = DAMPING * trace / BLOCK
    energy = jnp.sum(t0[...] * t0[...], keepdims=True)
    norm = jnp.sqrt(energy + 2.0 * shift * trace + BLOCK * shift * shift)
    for at in blocks:
        t0[at, at] = t0[at, at] + jnp.where(eye(128), shift, 0.0)
    scaled = t0[...] * (1.0 / norm)
    m0[...] = scaled
    b0[...] = scaled.astype(BF16)

    bands = [pl.ds(256 * i, 256) for i in range(BLOCK // 256)]

    def newton(m, m_half, m_next, next_half):
        for at in bands:
            b1[at] = (nn(m_half[at], m_half[...]) * 0.0625 - 0.625 * m[at]).astype(BF16)
        for at in bands:
            product = 1.5625 * m[at] + nn(b1[at], m_half[...])
            t0[at] = product
            xr[at] = product.astype(BF16)
        for at in bands:
            product = 1.5625 * t0[at] + nn(b1[at], xr[...])
            m_next[at] = product
            next_half[at] = product.astype(BF16)

    newton(m0, b0, m1, b2)
    newton(m1, b2, m2, b3)

    scale = lax.rsqrt(jnp.sqrt(norm))
    give_half = remote(hbuf, hbuf, ex_send, ex_recv, sibling)

    @pl.when(core == 0)
    def _():
        starts = [pl.multiple_of((x_ * 2 + zl) * 64, 64) for x_ in (x, x_mirror)]

        def slabs(ref):
            return jnp.concatenate([ref[pl.ds(start, 64), :] for start in starts], axis=0)

        g = nn(slabs(b0), b2[...]) * 0.0625 - 0.3125 * (slabs(m0) + slabs(m1))
        root = 1.25 * g - 0.390625 * slabs(m2) - 0.25 * nn(g.astype(BF16), b3[...])
        row = lax.broadcasted_iota(jnp.int32, (128, BLOCK), 0)
        row = jnp.where(row < 64, row + starts[0], row + (starts[1] - 64))
        column = lax.broadcasted_iota(jnp.int32, (128, BLOCK), 1)
        root = (root + jnp.where(row == column, 1.953125, 0.0)) * scale
        hbuf[...] = nn(root.astype(BF16), u_ref[...]).astype(BF16)
        give_half.start()
        give_half.wait_send()

    @pl.when(core == 1)
    def _():
        for at in bands:
            g = nn(b0[at], b2[...]) * 0.0625 - 0.3125 * (m0[at] + m1[at])
            t0[at] = g
            b1[at] = g.astype(BF16)
        for half in range(2):
            at = pl.ds(half * HALF, HALF)
            root = 1.25 * t0[:, at] - 0.390625 * m2[:, at] - 0.25 * nn(b1[...], b3[:, at])
            t0[:, at] = root
            t0[at, at] = t0[at, at] + jnp.where(eye(HALF), 1.953125, 0.0)
            xr[:, at] = (t0[:, at] * scale).astype(BF16)
        give_half.wait_recv()
        piece = (nn(hbuf[...], xr[...]) * math.sqrt(BLOCK)).astype(BF16)
        osrc[0] = piece[0:64]
        osrc[1] = piece[64:128]

    def place(row_block, cb):
        lanes = pl.ds(pl.multiple_of(cb * BLOCK, BLOCK), BLOCK)
        return upd_ref.at[row_block, :, lanes]

    def landing(dx, dy):
        return place(lax.rem(y + 8 - dy, 8), 1 - c if dx else c)

    def send_out(dx, dy):
        remote(osrc.at[dx], place(y, c), o_send, o_recv.at[dx, dy], out_peer(dx, dy)).start()

    def take(dx, dy):
        landed = landing(dx, dy)
        remote(landed, landed, o_send, o_recv.at[dx, dy], sibling).wait_recv()

    def share(dx, dy):
        landed = landing(dx, dy)
        remote(landed, landed, of_send, of_recv, sibling).start()

    def hand_on(dx, dy, step):
        landed = landing(dx, dy)
        remote(
            landed, landed, o_send, o_recv.at[dx, (dy + step) % 8], out_peer(0, step % 8)
        ).start()

    @pl.when(core == 1)
    def _():
        for dx, dy in ((1, 2), (1, 6), (0, 2), (0, 6), (1, 1), (1, 7), (0, 1), (0, 7), (1, 0)):
            send_out(dx, dy)
        remote(osrc.at[0], place(y, c), of_send, of_recv, sibling).start()
        place(y, c)[...] = osrc[0]
        for dx, dy, step in ((0, 2, 1), (0, 6, -1), (1, 2, 1), (1, 6, -1)):
            take(dx, dy)
            if dx == (dy == 6):
                hand_on(dx, dy, 2 * step)
            hand_on(dx, dy, step)
            share(dx, dy)
        for dx, dy in ((1, 0), (0, 1), (0, 7), (1, 1), (1, 7), (0, 3), (0, 5), (1, 3), (1, 5), (0, 4), (1, 4)):
            take(dx, dy)
            share(dx, dy)
        for sent in [tile.at[0]] * 3 + [tile.at[0, 0], tile.at[0, 0, pl.ds(0, 2)]]:
            remote(sent, sent, o_send, th_recv.at[0, 0], sibling).wait_send()
        remote(upd_ref, upd_ref, of_send, of_recv, sibling).wait_send()

    @pl.when(core == 0)
    def _():
        remote(upd_ref, upd_ref, of_send, of_recv, sibling).wait_recv()

    for half in range(2):
        all_z2 = z2.at[half, pl.ds(0, 7)]
        three = y2.at[half, pl.ds(0, 3)]
        all_zg = z1.at[half, :, pl.ds(0, 5)]
        for sent, sem in (
            (y1.at[half], y1_send), (z1.at[half], z1_send), (all_z2, z2_send),
            (three, y2_send), (three, yg_send), (all_zg, zg_send),
        ):
            remote(sent, sent, sem.at[half], th_recv.at[0, 0], sibling).wait_send()


def drain(out_vmem, upd_vmem, out_hbm, upd_hbm, sem):
    copies = [pltpu.make_async_copy(out_vmem, out_hbm, sem.at[8])]
    copies += [pltpu.make_async_copy(upd_vmem.at[i], upd_hbm.at[i], sem.at[i]) for i in range(8)]
    for copy in copies:
        copy.start()
    for copy in copies:
        copy.wait()


def on_device(inputs, weight, cotangent):
    square = (BLOCK, BLOCK)
    dma = pltpu.SemaphoreType.DMA
    results = pl.pallas_call(
        kernel,
        out_shape=(
            pltpu.VMEM((128, 128), BF16),
            pltpu.VMEM((8, 64, CB * BLOCK), BF16),
        ),
        in_specs=[pl.BlockSpec(memory_space=pltpu.HBM)] * 3,
        out_specs=(pl.BlockSpec(memory_space=pltpu.VMEM),) * 2,
        scratch_shapes=[
            pltpu.VMEM((128, D), BF16),
            pltpu.VMEM((D, 128), BF16),
            pltpu.VMEM((128, 128), BF16),
            pltpu.VMEM((2, 8, 128, 128), BF16),
            pltpu.VMEM((2, 8, 128, 128), BF16),
            pltpu.VMEM((8, 128, HALF), F32),
            pltpu.VMEM((2, 8, 4, 16, 128), BF16),
            pltpu.VMEM((2, 4, 8, 16, 128), BF16),
            pltpu.VMEM((2, 7, 4, 16, 128), BF16),
            pltpu.VMEM((2, 3, 8, 16, 128), BF16),
            pltpu.VMEM((2, 8, 16, 128), BF16),
            pltpu.VMEM((2, 8, 16, 128), BF16),
            pltpu.VMEM((2, 4, 4, 16, 128), BF16),
            pltpu.VMEM((2, 2, 4, 4, 2, 16, 128), BF16),
            pltpu.VMEM(square, BF16),
            pltpu.VMEM(square, F32),
            pltpu.VMEM(square, F32),
            pltpu.VMEM(square, F32),
            pltpu.VMEM(square, F32),
            pltpu.VMEM(square, BF16),
            pltpu.VMEM(square, BF16),
            pltpu.VMEM(square, BF16),
            pltpu.VMEM(square, BF16),
            pltpu.VMEM(square, BF16),
            pltpu.VMEM((128, BLOCK), BF16),
            pltpu.VMEM((2, 64, BLOCK), BF16),
            dma((10,)),
            dma((2, 4)), dma((2, 4)),
            *[dma((2,))] * 12,
            dma((2, 2)), dma((2, 2)), dma, dma,
            dma, dma((2, 8)), dma, dma,
        ],
        compiler_params=pltpu.CompilerParams(
            collective_id=0, has_side_effects=True, vmem_limit_bytes=48 * 2**20
        ),
    )(*(pltpu.with_memory_space_constraint(v, pltpu.HBM) for v in (inputs, weight, cotangent)))
    return pl.pallas_call(
        drain,
        out_shape=(
            jax.ShapeDtypeStruct((128, 128), BF16),
            jax.ShapeDtypeStruct((8, 64, CB * BLOCK), BF16),
        ),
        in_specs=[pl.BlockSpec(memory_space=pltpu.VMEM)] * 2,
        out_specs=(pl.BlockSpec(memory_space=pl.ANY),) * 2,
        scratch_shapes=[dma((9,))],
    )(*(pltpu.with_memory_space_constraint(v, pltpu.VMEM) for v in results))


def solution(mesh):
    placed = (P("dp", None), P(None, "pre"), P("dp", "pre"))
    return jax.shard_map(
        on_device,
        mesh=mesh,
        in_specs=placed,
        out_specs=(P("dp", "pre"), P(None, "pre", None)),
        check_vma=False,
    )
```

```python
import math

import jax
import jax.numpy as jnp
from jax import lax
from jax.experimental import pallas as pl
from jax.experimental.pallas import tpu as pltpu
from jax.sharding import PartitionSpec as P

D = 4096
BLOCK = 512
CB = 2
HALF = BLOCK // 2
DAMPING = 0.1
MESH = pl.DeviceIdType.MESH
BF16 = jnp.bfloat16
F32 = jnp.float32

Y_ORDER = (4, 3, 5, 2, 6, 1, 7, 0)


def nn(a, b):
    return lax.dot_general(a, b, (((1,), (0,)), ((), ())), preferred_element_type=F32)


def nt(a, b):
    return lax.dot_general(a, b, (((1,), (1,)), ((), ())), preferred_element_type=F32)


def kernel(
    a_hbm, w_hbm, b_hbm, out_ref, upd_ref,
    a_v, w_v, b_v, give, got, kept, part, part_z, y1, z1, zs, z2, y2, tile, u_ref,
    m0, m1, m2, t0, b0, b1, b2, b3, xr, hbuf, osrc,
    load_sem, sw_send, sw_recv,
    y1_send, y1_recv, z1_send, z1_recv, z2_send, z2_recv, y2_send, y2_recv,
    yg_send, yg_recv, zg_send, zg_recv, th_send, th_recv, ex_send, ex_recv,
    o_send, o_recv, of_send, of_recv,
):
    dp = lax.axis_index("dp")
    pre = lax.axis_index("pre")
    zh, y, core = lax.div(dp, 16), lax.rem(lax.div(dp, 2), 8), lax.rem(dp, 2)
    x, zl = lax.div(pre, 2), lax.rem(pre, 2)
    z = zh * 2 + zl
    c = lax.div(x, 2)
    x_pair = c * 2 + (1 - lax.rem(x, 2))
    x_mirror = 3 - x

    def dev(zh_, y_, core_, x_, zl_):
        return ((zh_ * 8 + y_) * 2 + core_, x_ * 2 + zl_)

    sibling = dev(zh, y, 1 - core, x, zl)

    def y_peer(dy):
        return dev(zh, lax.rem(y + dy, 8), core, x, zl)

    def z_peer(dzh):
        return dev(lax.rem(zh + dzh, 4), y, core, x, zl)

    def ag_peer(dx, dz):
        z_ = lax.rem(z + dz, 8)
        return dev(lax.div(z_, 2), y, core, x_pair if dx else x, lax.rem(z_, 2))

    def out_peer(dx, dy):
        return dev(zh, lax.rem(y + dy, 8), core, x_mirror if dx else x, zl)

    def remote(src, dst, send, recv, device):
        return pltpu.make_async_remote_copy(
            src_ref=src, dst_ref=dst, send_sem=send, recv_sem=recv,
            device_id=device, device_id_type=MESH,
        )

    def load_a(i):
        at = pl.ds(pl.multiple_of(lax.rem(y + Y_ORDER[i], 8) * BLOCK, BLOCK), BLOCK)
        return pltpu.make_async_copy(a_hbm.at[:, at], a_v.at[:, at], load_sem.at[i])

    load_b = pltpu.make_async_copy(b_hbm, b_v, load_sem.at[8])
    load_w = pltpu.make_async_copy(w_hbm, w_v, load_sem.at[9])
    load_b.start()
    for i in range(8):
        load_a(i).start()

    barrier = pltpu.get_barrier_semaphore()
    greeted = [ag_peer(dx, dz) for dz in (4, 3, 5, 2, 6, 1, 7, 0) for dx in (1, 0) if dx or dz]
    greeted += [y_peer(dy) for dy in Y_ORDER if dy]
    greeted += [out_peer(1, dy) for dy in (2, 6, 1, 7, 0)]
    greeted += [sibling]
    for device in greeted:
        pl.semaphore_signal(barrier, inc=1, device_id=device, device_id_type=MESH)

    def columns(dy, half):
        return pl.ds(pl.multiple_of(lax.rem(y + dy, 8) * BLOCK + half * HALF, HALF), HALF)

    load_b.wait()
    b_t = b_v[...].astype(F32).T.astype(BF16)
    b_t = jnp.concatenate(
        [b_t[h * 32 + path * 16 : h * 32 + path * 16 + 16] for path in range(2) for h in range(4)],
        axis=0,
    )
    for i, dy in enumerate(Y_ORDER):
        load_a(i).wait()
        terms = nn(b_t, a_v[:, columns(dy, 1 - core)]).astype(BF16)
        give[0, i] = terms[:, 0:128]
        give[1, i] = terms[:, 128:HALF]
        kept[i] = nn(b_t, a_v[:, columns(dy, core)])
    load_w.start()
    pl.semaphore_wait(barrier, len(greeted))

    def swap(half, pair):
        some = pl.ds(2 * pair, 2)
        return remote(
            give.at[half, some], got.at[half, some], sw_send.at[half, pair], sw_recv.at[half, pair],
            sibling,
        )

    for pair in range(4):
        swap(0, pair).start()

    def send_y(half, i):
        remote(
            part.at[half, i], y1.at[half, i], y1_send.at[half], y1_recv.at[half], y_peer(Y_ORDER[i])
        ).start()

    def send_z(half, first, count):
        some = pl.ds(first, count)
        for dzh in (2, 1, 3):
            remote(
                part_z.at[half, lax.rem(zh + dzh, 4), some], z1.at[half, dzh - 1, some],
                z1_send.at[half], z1_recv.at[half], z_peer(dzh),
            ).start()

    for half in range(2):
        for pair in range(4):
            swap(half, pair).wait()
            for i in (2 * pair, 2 * pair + 1):
                lanes = pl.ds(half * 128, 128)
                terms = (kept[i, :, lanes] + got[half, i].astype(F32)).astype(BF16)
                terms = terms.reshape(2, 4, 16, 128)
                part[half, i] = terms[0]
                part_z[half, :, i] = terms[1]
            if half == 0:
                send_z(half, 2 * pair, 2)
                swap(1, pair).start()
                for i in (2 * pair, 2 * pair + 1):
                    if Y_ORDER[i]:
                        send_y(half, i)
            else:
                if pair % 2:
                    send_z(half, 2 * pair - 2, 4)
                for i in (2 * pair, 2 * pair + 1):
                    if Y_ORDER[i]:
                        send_y(half, i)

    load_w.wait()
    out_ref[...] = nn(a_v[...], w_v[...]).astype(BF16)

    for half in range(2):
        remote(z1.at[half], z1.at[half], z1_send.at[half], z1_recv.at[half], sibling).wait_recv()
        for i, dy in enumerate(Y_ORDER):
            terms = part_z[half, zh, i].astype(F32)
            for dzh in range(3):
                terms += z1[half, dzh, i].astype(F32)
            zs[half, i] = terms.astype(BF16)
            if dy:
                remote(
                    zs.at[half, i], z2.at[half, i], z2_send.at[half], z2_recv.at[half], y_peer(dy)
                ).start()
        remote(y1.at[half], y1.at[half], y1_send.at[half], y1_recv.at[half], sibling).wait_recv()
        total = part[half, 7].astype(F32)
        for i in range(7):
            total += y1[half, i].astype(F32)
        y2[half, zh] = total.astype(BF16)
        for dzh in (2, 1, 3):
            own = y2.at[half, zh]
            remote(own, own, y2_send.at[half], y2_recv.at[half], z_peer(dzh)).start()

    mine = lax.rem(x, 2) * 2 + zl
    for half in range(2):
        all_z2 = z2.at[half, pl.ds(0, 7)]
        remote(all_z2, all_z2, z2_send.at[half], z2_recv.at[half], sibling).wait_recv()
        total = zs[half, 7].astype(F32)
        for i in range(7):
            total += z2[half, i].astype(F32)
        tile[core, half, mine, zh, 1] = total.astype(BF16)
        piece = tile.at[core, half, mine, zh, 1]
        for dz in (4, 3, 5, 2, 6, 1, 7, 0):
            for dx in (1, 0):
                if dx or dz:
                    remote(
                        piece, piece, zg_send.at[half], zg_recv.at[half], ag_peer(dx, dz)
                    ).start()
        three = y2.at[half, pl.ds(0, 3)]
        remote(three, three, y2_send.at[half], y2_recv.at[half], sibling).wait_recv()
        total = y2[half, 0].astype(F32)
        for h in range(1, 4):
            total += y2[half, h].astype(F32)
        tile[core, half, mine, :, 0] = total.astype(BF16)
        piece = tile.at[core, half, mine, :, 0]
        for x_, zl_ in ((x_pair, 1 - zl), (x_pair, zl), (x, 1 - zl)):
            remote(
                piece, piece, yg_send.at[half], yg_recv.at[half], dev(zh, y, core, x_, zl_)
            ).start()

    def swap_tile(half, path):
        ref = tile.at[core, half, :, :, path]
        return remote(ref, ref, th_send.at[half, path], th_recv.at[half, path], sibling)

    for half in range(2):
        three = y2.at[half, pl.ds(0, 3)]
        remote(three, three, yg_send.at[half], yg_recv.at[half], sibling).wait_recv()
        swap_tile(half, 0).start()
        all_zg = z1.at[half, :, pl.ds(0, 5)]
        remote(all_zg, all_zg, zg_send.at[half], zg_recv.at[half], sibling).wait_recv()
        swap_tile(half, 1).start()
    for half in range(2):
        for path in range(2):
            swap_tile(half, path).wait()

    @pl.when(core == 0)
    def _():
        for i in range(4):
            u_ref[i * 128 : i * 128 + 128, :] = tile[i // 2, i % 2].reshape(BLOCK, 128).T

    @pl.when(core == 1)
    def _():
        for i in range(4):
            u_ref[:, i * 128 : i * 128 + 128] = tile[i // 2, i % 2].reshape(BLOCK, 128)

    def eye(n):
        return lax.broadcasted_iota(jnp.int32, (n, n), 0) == lax.broadcasted_iota(
            jnp.int32, (n, n), 1
        )

    t0[...] = nt(u_ref[...], u_ref[...])
    blocks = [pl.ds(128 * i, 128) for i in range(4)]
    trace = sum(jnp.where(eye(128), t0[at, at], 0.0) for at in blocks)
    trace = jnp.sum(trace, keepdims=True)
    shift = DAMPING * trace / BLOCK
    energy = jnp.sum(t0[...] * t0[...], keepdims=True)
    norm = jnp.sqrt(energy + 2.0 * shift * trace + BLOCK * shift * shift)
    for at in blocks:
        t0[at, at] = t0[at, at] + jnp.where(eye(128), shift, 0.0)
    scaled = t0[...] * (1.0 / norm)
    m0[...] = scaled
    b0[...] = scaled.astype(BF16)

    bands = [pl.ds(256 * i, 256) for i in range(BLOCK // 256)]

    def square(m, m_half):
        for at in bands:
            b1[at] = (nn(m_half[at], m_half[...]) * 0.0625 - 0.625 * m[at]).astype(BF16)

    def fifth(m, m_half, m_next, next_half):
        for at in bands:
            product = 1.5625 * m[at] + nn(b1[at], m_half[...])
            t0[at] = product
            xr[at] = product.astype(BF16)
        for at in bands:
            product = 1.5625 * t0[at] + nn(b1[at], xr[...])
            m_next[at] = product
            next_half[at] = product.astype(BF16)

    square(m0, b0)
    fifth(m0, b0, m1, b2)
    square(m1, b2)

    scale = lax.rsqrt(jnp.sqrt(norm))
    give_half = remote(hbuf, hbuf, ex_send, ex_recv, sibling)

    @pl.when(core == 0)
    def _():
        starts = [pl.multiple_of((x_ * 2 + zl) * 64, 64) for x_ in (x, x_mirror)]

        def slabs(ref):
            return jnp.concatenate([ref[pl.ds(start, 64), :] for start in starts], axis=0)

        e = slabs(b1).astype(F32)
        g = nn(slabs(b0), b2[...]) * 0.0625 - 0.3125 * (slabs(m0) + slabs(m1))
        once = 1.5625 * (g + e) + nn(g.astype(BF16), b1[...])
        twice = 2.44140625 * e + 1.5625 * once + nn(once.astype(BF16), b1[...])
        last = 3.814697265625 * slabs(m1) + nn(twice.astype(BF16), b2[...])
        root = 1.25 * g - 0.25 * last
        row = lax.broadcasted_iota(jnp.int32, (128, BLOCK), 0)
        row = jnp.where(row < 64, row + starts[0], row + (starts[1] - 64))
        column = lax.broadcasted_iota(jnp.int32, (128, BLOCK), 1)
        root = (root + jnp.where(row == column, 1.953125, 0.0)) * scale
        hbuf[...] = nn(root.astype(BF16), u_ref[...]).astype(BF16)
        give_half.start()
        give_half.wait_send()

    @pl.when(core == 1)
    def _():
        fifth(m1, b2, m2, b3)
        for at in bands:
            g = nn(b0[at], b2[...]) * 0.0625 - 0.3125 * (m0[at] + m1[at])
            t0[at] = g
            b1[at] = g.astype(BF16)
        for half in range(2):
            at = pl.ds(half * HALF, HALF)
            root = 1.25 * t0[:, at] - 0.390625 * m2[:, at] - 0.25 * nn(b1[...], b3[:, at])
            t0[:, at] = root
            t0[at, at] = t0[at, at] + jnp.where(eye(HALF), 1.953125, 0.0)
            xr[:, at] = (t0[:, at] * scale).astype(BF16)
        give_half.wait_recv()
        piece = (nn(hbuf[...], xr[...]) * math.sqrt(BLOCK)).astype(BF16)
        osrc[0] = piece[0:64]
        osrc[1] = piece[64:128]

    def place(row_block, cb):
        lanes = pl.ds(pl.multiple_of(cb * BLOCK, BLOCK), BLOCK)
        return upd_ref.at[row_block, :, lanes]

    def landing(dx, dy):
        return place(lax.rem(y + 8 - dy, 8), 1 - c if dx else c)

    def send_out(dx, dy):
        remote(osrc.at[dx], place(y, c), o_send, o_recv.at[dx, dy], out_peer(dx, dy)).start()

    def take(dx, dy):
        landed = landing(dx, dy)
        remote(landed, landed, o_send, o_recv.at[dx, dy], sibling).wait_recv()

    def share(dx, dy):
        landed = landing(dx, dy)
        remote(landed, landed, of_send, of_recv, sibling).start()

    def hand_on(dx, dy, step):
        landed = landing(dx, dy)
        remote(
            landed, landed, o_send, o_recv.at[dx, (dy + step) % 8], out_peer(0, step % 8)
        ).start()

    @pl.when(core == 1)
    def _():
        for dx, dy in ((1, 2), (1, 6), (0, 2), (0, 6), (1, 1), (1, 7), (0, 1), (0, 7), (1, 0)):
            send_out(dx, dy)
        remote(osrc.at[0], place(y, c), of_send, of_recv, sibling).start()
        place(y, c)[...] = osrc[0]
        for dx, dy, step in ((0, 2, 1), (0, 6, -1), (1, 2, 1), (1, 6, -1)):
            take(dx, dy)
            if dx == (dy == 6):
                hand_on(dx, dy, 2 * step)
            hand_on(dx, dy, step)
            share(dx, dy)
        for dx, dy in ((1, 0), (0, 1), (0, 7), (1, 1), (1, 7), (0, 3), (0, 5), (1, 3), (1, 5), (0, 4), (1, 4)):
            take(dx, dy)
            share(dx, dy)
        for sent in [tile.at[0]] * 3 + [tile.at[0, 0], tile.at[0, 0, pl.ds(0, 2)]]:
            remote(sent, sent, o_send, th_recv.at[0, 0], sibling).wait_send()
        remote(upd_ref, upd_ref, of_send, of_recv, sibling).wait_send()

    @pl.when(core == 0)
    def _():
        remote(upd_ref, upd_ref, of_send, of_recv, sibling).wait_recv()

    for half in range(2):
        all_z2 = z2.at[half, pl.ds(0, 7)]
        three = y2.at[half, pl.ds(0, 3)]
        all_zg = z1.at[half, :, pl.ds(0, 5)]
        for sent, sem in (
            (y1.at[half], y1_send), (z1.at[half], z1_send), (all_z2, z2_send),
            (three, y2_send), (three, yg_send), (all_zg, zg_send),
        ):
            remote(sent, sent, sem.at[half], th_recv.at[0, 0], sibling).wait_send()


def drain(out_vmem, upd_vmem, out_hbm, upd_hbm, sem):
    copies = [pltpu.make_async_copy(out_vmem, out_hbm, sem.at[8])]
    copies += [pltpu.make_async_copy(upd_vmem.at[i], upd_hbm.at[i], sem.at[i]) for i in range(8)]
    for copy in copies:
        copy.start()
    for copy in copies:
        copy.wait()


def on_device(inputs, weight, cotangent):
    square = (BLOCK, BLOCK)
    dma = pltpu.SemaphoreType.DMA
    results = pl.pallas_call(
        kernel,
        out_shape=(
            pltpu.VMEM((128, 128), BF16),
            pltpu.VMEM((8, 64, CB * BLOCK), BF16),
        ),
        in_specs=[pl.BlockSpec(memory_space=pltpu.HBM)] * 3,
        out_specs=(pl.BlockSpec(memory_space=pltpu.VMEM),) * 2,
        scratch_shapes=[
            pltpu.VMEM((128, D), BF16),
            pltpu.VMEM((D, 128), BF16),
            pltpu.VMEM((128, 128), BF16),
            pltpu.VMEM((2, 8, 128, 128), BF16),
            pltpu.VMEM((2, 8, 128, 128), BF16),
            pltpu.VMEM((8, 128, HALF), F32),
            pltpu.VMEM((2, 8, 4, 16, 128), BF16),
            pltpu.VMEM((2, 4, 8, 16, 128), BF16),
            pltpu.VMEM((2, 7, 4, 16, 128), BF16),
            pltpu.VMEM((2, 3, 8, 16, 128), BF16),
            pltpu.VMEM((2, 8, 16, 128), BF16),
            pltpu.VMEM((2, 8, 16, 128), BF16),
            pltpu.VMEM((2, 4, 4, 16, 128), BF16),
            pltpu.VMEM((2, 2, 4, 4, 2, 16, 128), BF16),
            pltpu.VMEM(square, BF16),
            pltpu.VMEM(square, F32),
            pltpu.VMEM(square, F32),
            pltpu.VMEM(square, F32),
            pltpu.VMEM(square, F32),
            pltpu.VMEM(square, BF16),
            pltpu.VMEM(square, BF16),
            pltpu.VMEM(square, BF16),
            pltpu.VMEM(square, BF16),
            pltpu.VMEM(square, BF16),
            pltpu.VMEM((128, BLOCK), BF16),
            pltpu.VMEM((2, 64, BLOCK), BF16),
            dma((10,)),
            dma((2, 4)), dma((2, 4)),
            *[dma((2,))] * 12,
            dma((2, 2)), dma((2, 2)), dma, dma,
            dma, dma((2, 8)), dma, dma,
        ],
        compiler_params=pltpu.CompilerParams(
            collective_id=0, has_side_effects=True, vmem_limit_bytes=48 * 2**20
        ),
    )(*(pltpu.with_memory_space_constraint(v, pltpu.HBM) for v in (inputs, weight, cotangent)))
    return pl.pallas_call(
        drain,
        out_shape=(
            jax.ShapeDtypeStruct((128, 128), BF16),
            jax.ShapeDtypeStruct((8, 64, CB * BLOCK), BF16),
        ),
        in_specs=[pl.BlockSpec(memory_space=pltpu.VMEM)] * 2,
        out_specs=(pl.BlockSpec(memory_space=pl.ANY),) * 2,
        scratch_shapes=[dma((9,))],
    )(*(pltpu.with_memory_space_constraint(v, pltpu.VMEM) for v in results))


def solution(mesh):
    placed = (P("dp", None), P(None, "pre"), P("dp", "pre"))
    return jax.shard_map(
        on_device,
        mesh=mesh,
        in_specs=placed,
        out_specs=(P("dp", "pre"), P(None, "pre", None)),
        check_vma=False,
    )
```

```python
import math

import jax
import jax.numpy as jnp
from jax import lax
from jax.experimental import pallas as pl
from jax.experimental.pallas import tpu as pltpu
from jax.sharding import PartitionSpec as P

D = 4096
BLOCK = 512
CB = 2
HALF = BLOCK // 2
DAMPING = 0.1
MESH = pl.DeviceIdType.MESH
BF16 = jnp.bfloat16
F32 = jnp.float32

Y_ORDER = (4, 3, 5, 2, 6, 1, 7, 0)


def nn(a, b):
    return lax.dot_general(a, b, (((1,), (0,)), ((), ())), preferred_element_type=F32)


def nt(a, b):
    return lax.dot_general(a, b, (((1,), (1,)), ((), ())), preferred_element_type=F32)


def kernel(
    a_hbm, w_hbm, b_hbm, out_ref, upd_ref,
    a_v, w_v, b_v, give, got, kept, part, part_z, y1, z1, zs, z2, y2, tile, u_ref,
    m0, m1, m2, t0, b0, b1, b2, b3, xr, hbuf, osrc,
    load_sem, sw_send, sw_recv,
    y1_send, y1_recv, z1_send, z1_recv, z2_send, z2_recv, y2_send, y2_recv,
    yg_send, yg_recv, zg_send, zg_recv, th_send, th_recv, ex_send, ex_recv,
    o_send, o_recv, of_send, of_recv,
):
    dp = lax.axis_index("dp")
    pre = lax.axis_index("pre")
    zh, y, core = lax.div(dp, 16), lax.rem(lax.div(dp, 2), 8), lax.rem(dp, 2)
    x, zl = lax.div(pre, 2), lax.rem(pre, 2)
    z = zh * 2 + zl
    c = lax.div(x, 2)
    x_pair = c * 2 + (1 - lax.rem(x, 2))
    x_mirror = 3 - x

    def dev(zh_, y_, core_, x_, zl_):
        return ((zh_ * 8 + y_) * 2 + core_, x_ * 2 + zl_)

    sibling = dev(zh, y, 1 - core, x, zl)

    def y_peer(dy):
        return dev(zh, lax.rem(y + dy, 8), core, x, zl)

    def z_peer(dzh):
        return dev(lax.rem(zh + dzh, 4), y, core, x, zl)

    def ag_peer(dx, dz):
        z_ = lax.rem(z + dz, 8)
        return dev(lax.div(z_, 2), y, core, x_pair if dx else x, lax.rem(z_, 2))

    def out_peer(dx, dy):
        return dev(zh, lax.rem(y + dy, 8), core, x_mirror if dx else x, zl)

    def remote(src, dst, send, recv, device):
        return pltpu.make_async_remote_copy(
            src_ref=src, dst_ref=dst, send_sem=send, recv_sem=recv,
            device_id=device, device_id_type=MESH,
        )

    def load_a(i):
        at = pl.ds(pl.multiple_of(lax.rem(y + Y_ORDER[i], 8) * BLOCK, BLOCK), BLOCK)
        return pltpu.make_async_copy(a_hbm.at[:, at], a_v.at[:, at], load_sem.at[i])

    load_b = pltpu.make_async_copy(b_hbm, b_v, load_sem.at[8])
    load_w = pltpu.make_async_copy(w_hbm, w_v, load_sem.at[9])
    load_b.start()
    for i in range(8):
        load_a(i).start()

    barrier = pltpu.get_barrier_semaphore()
    greeted = [ag_peer(dx, dz) for dz in (4, 3, 5, 2, 6, 1, 7, 0) for dx in (1, 0) if dx or dz]
    greeted += [y_peer(dy) for dy in Y_ORDER if dy]
    greeted += [out_peer(1, dy) for dy in (2, 6, 1, 7, 0)]
    greeted += [sibling]
    for device in greeted:
        pl.semaphore_signal(barrier, inc=1, device_id=device, device_id_type=MESH)

    def columns(dy, half):
        return pl.ds(pl.multiple_of(lax.rem(y + dy, 8) * BLOCK + half * HALF, HALF), HALF)

    load_b.wait()
    b_t = b_v[...].astype(F32).T.astype(BF16)
    b_t = jnp.concatenate(
        [b_t[h * 32 + path * 16 : h * 32 + path * 16 + 16] for path in range(2) for h in range(4)],
        axis=0,
    )
    for i, dy in enumerate(Y_ORDER):
        load_a(i).wait()
        terms = nn(b_t, a_v[:, columns(dy, 1 - core)]).astype(BF16)
        give[0, i] = terms[:, 0:128]
        give[1, i] = terms[:, 128:HALF]
        kept[i] = nn(b_t, a_v[:, columns(dy, core)])
    load_w.start()
    pl.semaphore_wait(barrier, len(greeted))

    def swap(half, pair):
        some = pl.ds(2 * pair, 2)
        return remote(
            give.at[half, some], got.at[half, some], sw_send.at[half, pair], sw_recv.at[half, pair],
            sibling,
        )

    for pair in range(4):
        swap(0, pair).start()

    def send_y(half, i):
        remote(
            part.at[half, i], y1.at[half, i], y1_send.at[half], y1_recv.at[half], y_peer(Y_ORDER[i])
        ).start()

    def send_z(half, first, count):
        some = pl.ds(first, count)
        for dzh in (2, 1, 3):
            remote(
                part_z.at[half, lax.rem(zh + dzh, 4), some], z1.at[half, dzh - 1, some],
                z1_send.at[half], z1_recv.at[half], z_peer(dzh),
            ).start()

    for half in range(2):
        for pair in range(4):
            swap(half, pair).wait()
            for i in (2 * pair, 2 * pair + 1):
                lanes = pl.ds(half * 128, 128)
                terms = (kept[i, :, lanes] + got[half, i].astype(F32)).astype(BF16)
                terms = terms.reshape(2, 4, 16, 128)
                part[half, i] = terms[0]
                part_z[half, :, i] = terms[1]
            if half == 0:
                send_z(half, 2 * pair, 2)
                swap(1, pair).start()
                for i in (2 * pair, 2 * pair + 1):
                    if Y_ORDER[i]:
                        send_y(half, i)
            else:
                if pair % 2:
                    send_z(half, 2 * pair - 2, 4)
                for i in (2 * pair, 2 * pair + 1):
                    if Y_ORDER[i]:
                        send_y(half, i)

    load_w.wait()
    out_ref[...] = nn(a_v[...], w_v[...]).astype(BF16)

    for half in range(2):
        remote(z1.at[half], z1.at[half], z1_send.at[half], z1_recv.at[half], sibling).wait_recv()
        for i, dy in enumerate(Y_ORDER):
            terms = part_z[half, zh, i].astype(F32)
            for dzh in range(3):
                terms += z1[half, dzh, i].astype(F32)
            zs[half, i] = terms.astype(BF16)
            if dy:
                remote(
                    zs.at[half, i], z2.at[half, i], z2_send.at[half], z2_recv.at[half], y_peer(dy)
                ).start()
        remote(y1.at[half], y1.at[half], y1_send.at[half], y1_recv.at[half], sibling).wait_recv()
        total = part[half, 7].astype(F32)
        for i in range(7):
            total += y1[half, i].astype(F32)
        y2[half, zh] = total.astype(BF16)
        for dzh in (2, 1, 3):
            own = y2.at[half, zh]
            remote(own, own, y2_send.at[half], y2_recv.at[half], z_peer(dzh)).start()

    mine = lax.rem(x, 2) * 2 + zl
    for half in range(2):
        all_z2 = z2.at[half, pl.ds(0, 7)]
        remote(all_z2, all_z2, z2_send.at[half], z2_recv.at[half], sibling).wait_recv()
        total = zs[half, 7].astype(F32)
        for i in range(7):
            total += z2[half, i].astype(F32)
        tile[core, half, mine, zh, 1] = total.astype(BF16)
        piece = tile.at[core, half, mine, zh, 1]
        for dz in (4, 3, 5, 2, 6, 1, 7, 0):
            for dx in (1, 0):
                if dx or dz:
                    remote(
                        piece, piece, zg_send.at[half], zg_recv.at[half], ag_peer(dx, dz)
                    ).start()
        three = y2.at[half, pl.ds(0, 3)]
        remote(three, three, y2_send.at[half], y2_recv.at[half], sibling).wait_recv()
        total = y2[half, 0].astype(F32)
        for h in range(1, 4):
            total += y2[half, h].astype(F32)
        tile[core, half, mine, :, 0] = total.astype(BF16)
        piece = tile.at[core, half, mine, :, 0]
        for x_, zl_ in ((x_pair, 1 - zl), (x_pair, zl), (x, 1 - zl)):
            remote(
                piece, piece, yg_send.at[half], yg_recv.at[half], dev(zh, y, core, x_, zl_)
            ).start()

    def swap_tile(half, path):
        ref = tile.at[core, half, :, :, path]
        return remote(ref, ref, th_send.at[half, path], th_recv.at[half, path], sibling)

    for half in range(2):
        three = y2.at[half, pl.ds(0, 3)]
        remote(three, three, yg_send.at[half], yg_recv.at[half], sibling).wait_recv()
        swap_tile(half, 0).start()
        all_zg = z1.at[half, :, pl.ds(0, 5)]
        remote(all_zg, all_zg, zg_send.at[half], zg_recv.at[half], sibling).wait_recv()
        swap_tile(half, 1).start()
    for half in range(2):
        for path in range(2):
            swap_tile(half, path).wait()

    @pl.when(core == 0)
    def _():
        for i in range(4):
            u_ref[i * 128 : i * 128 + 128, :] = tile[i // 2, i % 2].reshape(BLOCK, 128).T

    @pl.when(core == 1)
    def _():
        for i in range(4):
            u_ref[:, i * 128 : i * 128 + 128] = tile[i // 2, i % 2].reshape(BLOCK, 128)

    def eye(n):
        return lax.broadcasted_iota(jnp.int32, (n, n), 0) == lax.broadcasted_iota(
            jnp.int32, (n, n), 1
        )

    t0[...] = nt(u_ref[...], u_ref[...])
    blocks = [pl.ds(128 * i, 128) for i in range(4)]
    trace = sum(jnp.where(eye(128), t0[at, at], 0.0) for at in blocks)
    trace = jnp.sum(trace, keepdims=True)
    shift = DAMPING * trace / BLOCK
    energy = jnp.sum(t0[...] * t0[...], keepdims=True)
    norm = jnp.sqrt(energy + 2.0 * shift * trace + BLOCK * shift * shift)
    for at in blocks:
        t0[at, at] = t0[at, at] + jnp.where(eye(128), shift, 0.0)
    scaled = t0[...] * (1.0 / norm)
    m0[...] = scaled
    b0[...] = scaled.astype(BF16)

    bands = [pl.ds(256 * i, 256) for i in range(BLOCK // 256)]

    def square(m, m_half):
        for at in bands:
            b1[at] = (nn(m_half[at], m_half[...]) * 0.0625 - 0.625 * m[at]).astype(BF16)

    def fifth(m, m_half, m_next, next_half):
        for at in bands:
            product = 1.5625 * m[at] + nn(b1[at], m_half[...])
            t0[at] = product
            xr[at] = product.astype(BF16)
        for at in bands:
            product = 1.5625 * t0[at] + nn(b1[at], xr[...])
            m_next[at] = product
            next_half[at] = product.astype(BF16)

    square(m0, b0)
    fifth(m0, b0, m1, b2)
    square(m1, b2)

    scale = lax.rsqrt(jnp.sqrt(norm))
    def give_half(slab):
        rows = hbuf.at[pl.ds(slab * 64, 64)]
        return remote(rows, rows, ex_send.at[slab], ex_recv.at[slab], sibling)


    @pl.when(core == 0)
    def _():
        starts = [pl.multiple_of((x_ * 2 + zl) * 64, 64) for x_ in (x, x_mirror)]

        def slabs(ref):
            return jnp.concatenate([ref[pl.ds(start, 64), :] for start in starts], axis=0)

        e = slabs(b1).astype(F32)
        g = nn(slabs(b0), b2[...]) * 0.0625 - 0.3125 * (slabs(m0) + slabs(m1))
        once = 1.5625 * (g + e) + nn(g.astype(BF16), b1[...])
        twice = 2.44140625 * e + 1.5625 * once + nn(once.astype(BF16), b1[...])
        last = 3.814697265625 * slabs(m1) + nn(twice.astype(BF16), b2[...])
        root = 1.25 * g - 0.25 * last
        row = lax.broadcasted_iota(jnp.int32, (128, BLOCK), 0)
        row = jnp.where(row < 64, row + starts[0], row + (starts[1] - 64))
        column = lax.broadcasted_iota(jnp.int32, (128, BLOCK), 1)
        root = (root + jnp.where(row == column, 1.953125, 0.0)) * scale
        root = root.astype(BF16)
        for slab in (1, 0):
            at = slice(slab * 64, slab * 64 + 64)
            hbuf[at] = nn(root[at], u_ref[...]).astype(BF16)
            give_half(slab).start()
        for slab in (1, 0):
            give_half(slab).wait_send()

    @pl.when(core == 1)
    def _():
        fifth(m1, b2, m2, b3)
        for at in bands:
            g = nn(b0[at], b2[...]) * 0.0625 - 0.3125 * (m0[at] + m1[at])
            t0[at] = g
            b1[at] = g.astype(BF16)
        for half in range(2):
            at = pl.ds(half * HALF, HALF)
            root = 1.25 * t0[:, at] - 0.390625 * m2[:, at] - 0.25 * nn(b1[...], b3[:, at])
            t0[:, at] = root
            t0[at, at] = t0[at, at] + jnp.where(eye(HALF), 1.953125, 0.0)
            xr[:, at] = (t0[:, at] * scale).astype(BF16)

    def place(row_block, cb):
        lanes = pl.ds(pl.multiple_of(cb * BLOCK, BLOCK), BLOCK)
        return upd_ref.at[row_block, :, lanes]

    def landing(dx, dy):
        return place(lax.rem(y + 8 - dy, 8), 1 - c if dx else c)

    def send_out(dx, dy):
        remote(osrc.at[dx], place(y, c), o_send, o_recv.at[dx, dy], out_peer(dx, dy)).start()

    def take(dx, dy):
        landed = landing(dx, dy)
        remote(landed, landed, o_send, o_recv.at[dx, dy], sibling).wait_recv()

    def share(dx, dy):
        landed = landing(dx, dy)
        remote(landed, landed, of_send, of_recv, sibling).start()

    def hand_on(dx, dy, step):
        landed = landing(dx, dy)
        remote(
            landed, landed, o_send, o_recv.at[dx, (dy + step) % 8], out_peer(0, step % 8)
        ).start()

    @pl.when(core == 1)
    def _():
        for slab in (1, 0):
            give_half(slab).wait_recv()
            piece = nn(hbuf[slab * 64 : slab * 64 + 64], xr[...]) * math.sqrt(BLOCK)
            osrc[slab] = piece.astype(BF16)
            send_out(slab, 2)
            send_out(slab, 6)
        for dx, dy in ((1, 1), (1, 7), (0, 1), (0, 7), (1, 0)):
            send_out(dx, dy)
        remote(osrc.at[0], place(y, c), of_send, of_recv, sibling).start()
        place(y, c)[...] = osrc[0]
        for dx, dy, step in ((0, 2, 1), (0, 6, -1), (1, 2, 1), (1, 6, -1)):
            take(dx, dy)
            if dx == (dy == 6):
                hand_on(dx, dy, 2 * step)
            hand_on(dx, dy, step)
            share(dx, dy)
        for dx, dy in ((1, 0), (0, 1), (0, 7), (1, 1), (1, 7), (0, 3), (0, 5), (1, 3), (1, 5), (0, 4), (1, 4)):
            take(dx, dy)
            share(dx, dy)
        for sent in [tile.at[0]] * 3 + [tile.at[0, 0], tile.at[0, 0, pl.ds(0, 2)]]:
            remote(sent, sent, o_send, th_recv.at[0, 0], sibling).wait_send()
        remote(upd_ref, upd_ref, of_send, of_recv, sibling).wait_send()

    @pl.when(core == 0)
    def _():
        remote(upd_ref, upd_ref, of_send, of_recv, sibling).wait_recv()

    for half in range(2):
        all_z2 = z2.at[half, pl.ds(0, 7)]
        three = y2.at[half, pl.ds(0, 3)]
        all_zg = z1.at[half, :, pl.ds(0, 5)]
        for sent, sem in (
            (y1.at[half], y1_send), (z1.at[half], z1_send), (all_z2, z2_send),
            (three, y2_send), (three, yg_send), (all_zg, zg_send),
        ):
            remote(sent, sent, sem.at[half], th_recv.at[0, 0], sibling).wait_send()


def drain(out_vmem, upd_vmem, out_hbm, upd_hbm, sem):
    copies = [pltpu.make_async_copy(out_vmem, out_hbm, sem.at[8])]
    copies += [pltpu.make_async_copy(upd_vmem.at[i], upd_hbm.at[i], sem.at[i]) for i in range(8)]
    for copy in copies:
        copy.start()
    for copy in copies:
        copy.wait()


def on_device(inputs, weight, cotangent):
    square = (BLOCK, BLOCK)
    dma = pltpu.SemaphoreType.DMA
    results = pl.pallas_call(
        kernel,
        out_shape=(
            pltpu.VMEM((128, 128), BF16),
            pltpu.VMEM((8, 64, CB * BLOCK), BF16),
        ),
        in_specs=[pl.BlockSpec(memory_space=pltpu.HBM)] * 3,
        out_specs=(pl.BlockSpec(memory_space=pltpu.VMEM),) * 2,
        scratch_shapes=[
            pltpu.VMEM((128, D), BF16),
            pltpu.VMEM((D, 128), BF16),
            pltpu.VMEM((128, 128), BF16),
            pltpu.VMEM((2, 8, 128, 128), BF16),
            pltpu.VMEM((2, 8, 128, 128), BF16),
            pltpu.VMEM((8, 128, HALF), F32),
            pltpu.VMEM((2, 8, 4, 16, 128), BF16),
            pltpu.VMEM((2, 4, 8, 16, 128), BF16),
            pltpu.VMEM((2, 7, 4, 16, 128), BF16),
            pltpu.VMEM((2, 3, 8, 16, 128), BF16),
            pltpu.VMEM((2, 8, 16, 128), BF16),
            pltpu.VMEM((2, 8, 16, 128), BF16),
            pltpu.VMEM((2, 4, 4, 16, 128), BF16),
            pltpu.VMEM((2, 2, 4, 4, 2, 16, 128), BF16),
            pltpu.VMEM(square, BF16),
            pltpu.VMEM(square, F32),
            pltpu.VMEM(square, F32),
            pltpu.VMEM(square, F32),
            pltpu.VMEM(square, F32),
            pltpu.VMEM(square, BF16),
            pltpu.VMEM(square, BF16),
            pltpu.VMEM(square, BF16),
            pltpu.VMEM(square, BF16),
            pltpu.VMEM(square, BF16),
            pltpu.VMEM((128, BLOCK), BF16),
            pltpu.VMEM((2, 64, BLOCK), BF16),
            dma((10,)),
            dma((2, 4)), dma((2, 4)),
            *[dma((2,))] * 12,
            dma((2, 2)), dma((2, 2)), dma((2,)), dma((2,)),
            dma, dma((2, 8)), dma, dma,
        ],
        compiler_params=pltpu.CompilerParams(
            collective_id=0, has_side_effects=True, vmem_limit_bytes=48 * 2**20
        ),
    )(*(pltpu.with_memory_space_constraint(v, pltpu.HBM) for v in (inputs, weight, cotangent)))
    return pl.pallas_call(
        drain,
        out_shape=(
            jax.ShapeDtypeStruct((128, 128), BF16),
            jax.ShapeDtypeStruct((8, 64, CB * BLOCK), BF16),
        ),
        in_specs=[pl.BlockSpec(memory_space=pltpu.VMEM)] * 2,
        out_specs=(pl.BlockSpec(memory_space=pl.ANY),) * 2,
        scratch_shapes=[dma((9,))],
    )(*(pltpu.with_memory_space_constraint(v, pltpu.VMEM) for v in results))


def solution(mesh):
    placed = (P("dp", None), P(None, "pre"), P("dp", "pre"))
    return jax.shard_map(
        on_device,
        mesh=mesh,
        in_specs=placed,
        out_specs=(P("dp", "pre"), P(None, "pre", None)),
        check_vma=False,
    )
```

```python
import math

import jax
import jax.numpy as jnp
from jax import lax
from jax.experimental import pallas as pl
from jax.experimental.pallas import tpu as pltpu
from jax.sharding import PartitionSpec as P

D = 4096
BLOCK = 512
CB = 2
HALF = BLOCK // 2
DAMPING = 0.1
MESH = pl.DeviceIdType.MESH
BF16 = jnp.bfloat16
F32 = jnp.float32

Y_ORDER = (4, 3, 5, 2, 6, 1, 7, 0)


def nn(a, b):
    return lax.dot_general(a, b, (((1,), (0,)), ((), ())), preferred_element_type=F32)


def nt(a, b):
    return lax.dot_general(a, b, (((1,), (1,)), ((), ())), preferred_element_type=F32)


def kernel(
    a_hbm, w_hbm, b_hbm, out_ref, upd_ref,
    a_v, w_v, b_v, give, got, kept, part, part_z, y1, z1, zs, z2, y2, tile, u_ref,
    m0, m1, m2, t0, b0, b1, b2, b3, xr, hbuf, osrc,
    load_sem, sw_send, sw_recv,
    y1_send, y1_recv, z1_send, z1_recv, z2_send, z2_recv, y2_send, y2_recv,
    yg_send, yg_recv, zg_send, zg_recv, th_send, th_recv, ex_send, ex_recv,
    o_send, o_recv, of_send, of_recv,
):
    dp = lax.axis_index("dp")
    pre = lax.axis_index("pre")
    zh, y, core = lax.div(dp, 16), lax.rem(lax.div(dp, 2), 8), lax.rem(dp, 2)
    x, zl = lax.div(pre, 2), lax.rem(pre, 2)
    z = zh * 2 + zl
    c = lax.div(x, 2)
    x_pair = c * 2 + (1 - lax.rem(x, 2))
    x_mirror = 3 - x

    def dev(zh_, y_, core_, x_, zl_):
        return ((zh_ * 8 + y_) * 2 + core_, x_ * 2 + zl_)

    sibling = dev(zh, y, 1 - core, x, zl)

    def y_peer(dy):
        return dev(zh, lax.rem(y + dy, 8), core, x, zl)

    def z_peer(dzh):
        return dev(lax.rem(zh + dzh, 4), y, core, x, zl)

    def ag_peer(dx, dz):
        z_ = lax.rem(z + dz, 8)
        return dev(lax.div(z_, 2), y, core, x_pair if dx else x, lax.rem(z_, 2))

    def out_peer(dx, dy):
        return dev(zh, lax.rem(y + dy, 8), core, x_mirror if dx else x, zl)

    def remote(src, dst, send, recv, device):
        return pltpu.make_async_remote_copy(
            src_ref=src, dst_ref=dst, send_sem=send, recv_sem=recv,
            device_id=device, device_id_type=MESH,
        )

    def load_a(i):
        at = pl.ds(pl.multiple_of(lax.rem(y + Y_ORDER[i], 8) * BLOCK, BLOCK), BLOCK)
        return pltpu.make_async_copy(a_hbm.at[:, at], a_v.at[:, at], load_sem.at[i])

    load_b = pltpu.make_async_copy(b_hbm, b_v, load_sem.at[8])
    load_w = pltpu.make_async_copy(w_hbm, w_v, load_sem.at[9])
    load_b.start()
    for i in range(8):
        load_a(i).start()

    barrier = pltpu.get_barrier_semaphore()
    greeted = [ag_peer(dx, dz) for dz in (4, 3, 5, 2, 6, 1, 7, 0) for dx in (1, 0) if dx or dz]
    greeted += [y_peer(dy) for dy in Y_ORDER if dy]
    greeted += [out_peer(1, dy) for dy in (2, 6, 1, 7, 0)]
    greeted += [sibling]
    for device in greeted:
        pl.semaphore_signal(barrier, inc=1, device_id=device, device_id_type=MESH)

    def columns(dy, half):
        return pl.ds(pl.multiple_of(lax.rem(y + dy, 8) * BLOCK + half * HALF, HALF), HALF)

    load_b.wait()
    b_t = b_v[...].astype(F32).T.astype(BF16)
    b_t = jnp.concatenate(
        [b_t[h * 32 + path * 16 : h * 32 + path * 16 + 16] for path in range(2) for h in range(4)],
        axis=0,
    )
    for i, dy in enumerate(Y_ORDER):
        load_a(i).wait()
        terms = nn(b_t, a_v[:, columns(dy, 1 - core)]).astype(BF16)
        give[0, i] = terms[:, 0:128]
        give[1, i] = terms[:, 128:HALF]
        kept[i] = nn(b_t, a_v[:, columns(dy, core)])
    load_w.start()
    pl.semaphore_wait(barrier, len(greeted))

    def swap(half, pair):
        some = pl.ds(2 * pair, 2)
        return remote(
            give.at[half, some], got.at[half, some], sw_send.at[half, pair], sw_recv.at[half, pair],
            sibling,
        )

    for pair in range(4):
        swap(0, pair).start()

    def send_y(half, i):
        remote(
            part.at[half, i], y1.at[half, i], y1_send.at[half], y1_recv.at[half], y_peer(Y_ORDER[i])
        ).start()

    def send_z(half, first, count):
        some = pl.ds(first, count)
        for dzh in (2, 1, 3):
            remote(
                part_z.at[half, lax.rem(zh + dzh, 4), some], z1.at[half, dzh - 1, some],
                z1_send.at[half], z1_recv.at[half], z_peer(dzh),
            ).start()

    for half in range(2):
        for pair in range(4):
            swap(half, pair).wait()
            for i in (2 * pair, 2 * pair + 1):
                lanes = pl.ds(half * 128, 128)
                terms = (kept[i, :, lanes] + got[half, i].astype(F32)).astype(BF16)
                terms = terms.reshape(2, 4, 16, 128)
                part[half, i] = terms[0]
                part_z[half, :, i] = terms[1]
            if half == 0:
                send_z(half, 2 * pair, 2)
                swap(1, pair).start()
                for i in (2 * pair, 2 * pair + 1):
                    if Y_ORDER[i]:
                        send_y(half, i)
            else:
                if pair % 2:
                    send_z(half, 2 * pair - 2, 4)
                for i in (2 * pair, 2 * pair + 1):
                    if Y_ORDER[i]:
                        send_y(half, i)

    load_w.wait()
    out_ref[...] = nn(a_v[...], w_v[...]).astype(BF16)

    for half in range(2):
        remote(z1.at[half], z1.at[half], z1_send.at[half], z1_recv.at[half], sibling).wait_recv()
        for i, dy in enumerate(Y_ORDER):
            terms = part_z[half, zh, i].astype(F32)
            for dzh in range(3):
                terms += z1[half, dzh, i].astype(F32)
            zs[half, i] = terms.astype(BF16)
            if dy:
                remote(
                    zs.at[half, i], z2.at[half, i], z2_send.at[half], z2_recv.at[half], y_peer(dy)
                ).start()
        remote(y1.at[half], y1.at[half], y1_send.at[half], y1_recv.at[half], sibling).wait_recv()
        total = part[half, 7].astype(F32)
        for i in range(7):
            total += y1[half, i].astype(F32)
        y2[half, zh] = total.astype(BF16)
        for dzh in (2, 1, 3):
            own = y2.at[half, zh]
            remote(own, own, y2_send.at[half], y2_recv.at[half], z_peer(dzh)).start()

    mine = lax.rem(x, 2) * 2 + zl
    for half in range(2):
        all_z2 = z2.at[half, pl.ds(0, 7)]
        remote(all_z2, all_z2, z2_send.at[half], z2_recv.at[half], sibling).wait_recv()
        total = zs[half, 7].astype(F32)
        for i in range(7):
            total += z2[half, i].astype(F32)
        tile[core, half, mine, zh, 1] = total.astype(BF16)
        piece = tile.at[core, half, mine, zh, 1]
        for dz in (4, 3, 5, 2, 6, 1, 7, 0):
            for dx in (1, 0):
                if dx or dz:
                    remote(
                        piece, piece, zg_send.at[half], zg_recv.at[half], ag_peer(dx, dz)
                    ).start()
        three = y2.at[half, pl.ds(0, 3)]
        remote(three, three, y2_send.at[half], y2_recv.at[half], sibling).wait_recv()
        total = y2[half, 0].astype(F32)
        for h in range(1, 4):
            total += y2[half, h].astype(F32)
        tile[core, half, mine, :, 0] = total.astype(BF16)
        piece = tile.at[core, half, mine, :, 0]
        for x_, zl_ in ((x_pair, 1 - zl), (x_pair, zl), (x, 1 - zl)):
            remote(
                piece, piece, yg_send.at[half], yg_recv.at[half], dev(zh, y, core, x_, zl_)
            ).start()

    def swap_tile(half, path):
        ref = tile.at[core, half, :, :, path]
        return remote(ref, ref, th_send.at[half, path], th_recv.at[half, path], sibling)

    for half in range(2):
        three = y2.at[half, pl.ds(0, 3)]
        remote(three, three, yg_send.at[half], yg_recv.at[half], sibling).wait_recv()
        swap_tile(half, 0).start()
        all_zg = z1.at[half, :, pl.ds(0, 5)]
        remote(all_zg, all_zg, zg_send.at[half], zg_recv.at[half], sibling).wait_recv()
        swap_tile(half, 1).start()
    for half in range(2):
        for path in range(2):
            swap_tile(half, path).wait()

    @pl.when(core == 0)
    def _():
        for i in range(4):
            u_ref[i * 128 : i * 128 + 128, :] = tile[i // 2, i % 2].reshape(BLOCK, 128).T

    @pl.when(core == 1)
    def _():
        for i in range(4):
            u_ref[:, i * 128 : i * 128 + 128] = tile[i // 2, i % 2].reshape(BLOCK, 128)

    def eye(n):
        return lax.broadcasted_iota(jnp.int32, (n, n), 0) == lax.broadcasted_iota(
            jnp.int32, (n, n), 1
        )

    t0[...] = nt(u_ref[...], u_ref[...])
    blocks = [pl.ds(128 * i, 128) for i in range(4)]
    trace = sum(jnp.where(eye(128), t0[at, at], 0.0) for at in blocks)
    trace = jnp.sum(trace, keepdims=True)
    shift = DAMPING * trace / BLOCK
    energy = jnp.sum(t0[...] * t0[...], keepdims=True)
    norm = jnp.sqrt(energy + 2.0 * shift * trace + BLOCK * shift * shift)
    for at in blocks:
        t0[at, at] = t0[at, at] + jnp.where(eye(128), shift, 0.0)
    scaled = t0[...] * (1.0 / norm)
    m0[...] = scaled
    b0[...] = scaled.astype(BF16)

    bands = [pl.ds(256 * i, 256) for i in range(BLOCK // 256)]

    def square(m, m_half):
        for at in bands:
            b1[at] = (nn(m_half[at], m_half[...]) * 0.0625 - 0.625 * m[at]).astype(BF16)

    def fifth(m, m_half, m_next, next_half):
        for at in bands:
            product = 1.5625 * m[at] + nn(b1[at], m_half[...])
            t0[at] = product
            xr[at] = product.astype(BF16)
        for at in bands:
            product = 1.5625 * t0[at] + nn(b1[at], xr[...])
            m_next[at] = product
            next_half[at] = product.astype(BF16)

    square(m0, b0)
    fifth(m0, b0, m1, b2)
    square(m1, b2)

    scale = lax.rsqrt(jnp.sqrt(norm))
    give_half = remote(hbuf, hbuf, ex_send, ex_recv, sibling)

    @pl.when(core == 0)
    def _():
        starts = [pl.multiple_of((x_ * 2 + zl) * 64, 64) for x_ in (x, x_mirror)]

        def slabs(ref):
            return jnp.concatenate([ref[pl.ds(start, 64), :] for start in starts], axis=0)

        e = slabs(b1).astype(F32)
        g = nn(slabs(b0), b2[...]) * 0.0625 - 0.3125 * (slabs(m0) + slabs(m1))
        once = 1.5625 * (g + e) + nn(g.astype(BF16), b1[...])
        twice = 2.44140625 * e + 1.5625 * once + nn(once.astype(BF16), b1[...])
        last = 3.814697265625 * slabs(m1) + nn(twice.astype(BF16), b2[...])
        root = 1.25 * g - 0.25 * last
        row = lax.broadcasted_iota(jnp.int32, (128, BLOCK), 0)
        row = jnp.where(row < 64, row + starts[0], row + (starts[1] - 64))
        column = lax.broadcasted_iota(jnp.int32, (128, BLOCK), 1)
        root = (root + jnp.where(row == column, 1.953125, 0.0)) * scale
        hbuf[...] = nn(root.astype(BF16), u_ref[...]).astype(BF16)
        give_half.start()
        give_half.wait_send()

    @pl.when(core == 1)
    def _():
        fifth(m1, b2, m2, b3)
        for at in bands:
            g = nn(b0[at], b2[...]) * 0.0625 - 0.3125 * (m0[at] + m1[at])
            t0[at] = g
            b1[at] = g.astype(BF16)
        for half in range(2):
            at = pl.ds(half * HALF, HALF)
            root = 1.25 * t0[:, at] - 0.390625 * m2[:, at] - 0.25 * nn(b1[...], b3[:, at])
            t0[:, at] = root
            t0[at, at] = t0[at, at] + jnp.where(eye(HALF), 1.953125, 0.0)
            xr[:, at] = (t0[:, at] * scale).astype(BF16)
        give_half.wait_recv()
        piece = (nn(hbuf[...], xr[...]) * math.sqrt(BLOCK)).astype(BF16)
        osrc[0] = piece[0:64]
        osrc[1] = piece[64:128]

    def place(row_block, cb):
        lanes = pl.ds(pl.multiple_of(cb * BLOCK, BLOCK), BLOCK)
        return upd_ref.at[row_block, :, lanes]

    def landing(dx, dy):
        return place(lax.rem(y + 8 - dy, 8), 1 - c if dx else c)

    def send_out(dx, dy):
        remote(osrc.at[dx], place(y, c), o_send, o_recv.at[dx, dy], out_peer(dx, dy)).start()

    def take(dx, dy):
        landed = landing(dx, dy)
        remote(landed, landed, o_send, o_recv.at[dx, dy], sibling).wait_recv()

    def share(dx, dy):
        landed = landing(dx, dy)
        remote(landed, landed, of_send, of_recv, sibling).start()

    def hand_on(dx, dy, step):
        landed = landing(dx, dy)
        remote(
            landed, landed, o_send, o_recv.at[dx, (dy + step) % 8], out_peer(0, step % 8)
        ).start()

    @pl.when(core == 1)
    def _():
        for dx, dy in ((1, 2), (1, 6), (0, 2), (0, 6), (1, 1), (1, 7), (0, 1), (0, 7), (1, 0)):
            send_out(dx, dy)
        remote(osrc.at[0], place(y, c), of_send, of_recv, sibling).start()
        place(y, c)[...] = osrc[0]
        for dx, dy, step in ((0, 2, 1), (0, 6, -1), (1, 2, 1), (1, 6, -1)):
            take(dx, dy)
            if dx == (dy == 6):
                hand_on(dx, dy, 2 * step)
            hand_on(dx, dy, step)
            share(dx, dy)
        for dx, dy in ((1, 0), (0, 1), (0, 7), (1, 1), (1, 7), (0, 3), (0, 5), (1, 3), (1, 5), (0, 4), (1, 4)):
            take(dx, dy)
            share(dx, dy)
        for sent in [tile.at[0]] * 3 + [tile.at[0, 0], tile.at[0, 0, pl.ds(0, 2)]]:
            remote(sent, sent, o_send, th_recv.at[0, 0], sibling).wait_send()
        remote(upd_ref, upd_ref, of_send, of_recv, sibling).wait_send()

    @pl.when(core == 0)
    def _():
        remote(upd_ref, upd_ref, of_send, of_recv, sibling).wait_recv()

    for half in range(2):
        all_z2 = z2.at[half, pl.ds(0, 7)]
        three = y2.at[half, pl.ds(0, 3)]
        all_zg = z1.at[half, :, pl.ds(0, 5)]
        for sent, sem in (
            (y1.at[half], y1_send), (z1.at[half], z1_send), (all_z2, z2_send),
            (three, y2_send), (three, yg_send), (all_zg, zg_send),
        ):
            remote(sent, sent, sem.at[half], th_recv.at[0, 0], sibling).wait_send()


def drain(out_vmem, upd_vmem, out_hbm, upd_hbm, sem):
    copies = [pltpu.make_async_copy(out_vmem, out_hbm, sem.at[8])]
    for i in range(4):
        at = pl.ds(2 * i, 2)
        copies += [pltpu.make_async_copy(upd_vmem.at[at], upd_hbm.at[at], sem.at[i])]
    for copy in copies:
        copy.start()
    for copy in copies:
        copy.wait()


def on_device(inputs, weight, cotangent):
    square = (BLOCK, BLOCK)
    dma = pltpu.SemaphoreType.DMA
    results = pl.pallas_call(
        kernel,
        out_shape=(
            pltpu.VMEM((128, 128), BF16),
            pltpu.VMEM((8, 64, CB * BLOCK), BF16),
        ),
        in_specs=[pl.BlockSpec(memory_space=pltpu.HBM)] * 3,
        out_specs=(pl.BlockSpec(memory_space=pltpu.VMEM),) * 2,
        scratch_shapes=[
            pltpu.VMEM((128, D), BF16),
            pltpu.VMEM((D, 128), BF16),
            pltpu.VMEM((128, 128), BF16),
            pltpu.VMEM((2, 8, 128, 128), BF16),
            pltpu.VMEM((2, 8, 128, 128), BF16),
            pltpu.VMEM((8, 128, HALF), F32),
            pltpu.VMEM((2, 8, 4, 16, 128), BF16),
            pltpu.VMEM((2, 4, 8, 16, 128), BF16),
            pltpu.VMEM((2, 7, 4, 16, 128), BF16),
            pltpu.VMEM((2, 3, 8, 16, 128), BF16),
            pltpu.VMEM((2, 8, 16, 128), BF16),
            pltpu.VMEM((2, 8, 16, 128), BF16),
            pltpu.VMEM((2, 4, 4, 16, 128), BF16),
            pltpu.VMEM((2, 2, 4, 4, 2, 16, 128), BF16),
            pltpu.VMEM(square, BF16),
            pltpu.VMEM(square, F32),
            pltpu.VMEM(square, F32),
            pltpu.VMEM(square, F32),
            pltpu.VMEM(square, F32),
            pltpu.VMEM(square, BF16),
            pltpu.VMEM(square, BF16),
            pltpu.VMEM(square, BF16),
            pltpu.VMEM(square, BF16),
            pltpu.VMEM(square, BF16),
            pltpu.VMEM((128, BLOCK), BF16),
            pltpu.VMEM((2, 64, BLOCK), BF16),
            dma((10,)),
            dma((2, 4)), dma((2, 4)),
            *[dma((2,))] * 12,
            dma((2, 2)), dma((2, 2)), dma, dma,
            dma, dma((2, 8)), dma, dma,
        ],
        compiler_params=pltpu.CompilerParams(
            collective_id=0, has_side_effects=True, vmem_limit_bytes=48 * 2**20
        ),
    )(*(pltpu.with_memory_space_constraint(v, pltpu.HBM) for v in (inputs, weight, cotangent)))
    return pl.pallas_call(
        drain,
        out_shape=(
            jax.ShapeDtypeStruct((128, 128), BF16),
            jax.ShapeDtypeStruct((8, 64, CB * BLOCK), BF16),
        ),
        in_specs=[pl.BlockSpec(memory_space=pltpu.VMEM)] * 2,
        out_specs=(pl.BlockSpec(memory_space=pl.ANY),) * 2,
        scratch_shapes=[dma((9,))],
    )(*(pltpu.with_memory_space_constraint(v, pltpu.VMEM) for v in results))


def solution(mesh):
    placed = (P("dp", None), P(None, "pre"), P("dp", "pre"))
    return jax.shard_map(
        on_device,
        mesh=mesh,
        in_specs=placed,
        out_specs=(P("dp", "pre"), P(None, "pre", None)),
        check_vma=False,
    )
```
